256 devices in a mesh: dp: 8 (over x, core), context: 32 (over z, y).
Axes of the slice: x: 4, y: 4, z: 8, core: 2. Of those that a mesh axis runs over, the one named last changes fastest.
Arguments:
- hidden: bfloat16 [8, 24576, 8192], P('dp', 'context'), may hold values from -6 to 6
- norm_gain: bfloat16 [8192], P('context'), may hold values from 0.099609375 to 1.8984375
- w_in: bfloat16 [8192, 512], P('context'), may hold values from -0.0625 to 0.0625
- w_out: bfloat16 [512], replicated, may hold values from -0.25 to 0.25
- rewards: float32 [8, 49152], P('dp', 'context'), may hold values from -0.3125 to 0.3125
- old_values: float32 [8, 49152], P('dp', 'context'), may hold values from -6 to 6
- send_slot: int32 [8, 49152], P('dp', 'context'), may hold values from -1 to 1535, as said below
- pack_slot: int32 [8, 24576], P('dp', 'context'), may hold values from 0 to 1535, as said below
- positions: int32 [8, 24576], P('dp', 'context'), may hold values from 0 to 24575, as said below
- episode_len: int32 [8, 24576], P('dp', 'context'), may hold values from 1 to 24576, as said below
Outputs:
- advantages: float32 [8, 49152], P('dp', 'context')
- value_loss: float32 [8, 49152], P('dp', 'context')
The draws below stay inside these ranges and needn't reach their ends.
Inputs may be any that keep to these rules, and one draw needn't show every extreme that they name: `send_slot`: owner slot entries are r * 192 + k (the k-th token this owner shard sends to packed row r at the same context index) or -1 for an empty slot; for each owner shard and row the used k run from 0 without gaps, at most 192 of them; every packed shard receives exactly 768 tokens, a full 192 from at least one owner shard. `pack_slot`: entries are o * 192 + k, naming each (owner, k) sent to this packed shard exactly once; they match send_slot. Each packed row is a sequence of whole episodes; positions count 0, 1, 2, ... within each episode, starting at 0 at the row's first position. `episode_len`: equal to the number of positions of the episode that holds the token.
All inputs are finite; a program needn't handle non-finite values.
Results may differ from the reference program's by a relative error of at most 0.0042.
Values may be sent and summed in bfloat16 or wider, within the bound.
A program may use at most 128 MiB of HBM per device.

```python
import jax
import jax.numpy as jnp
from jax import lax

D = 8192
VH = 512
CTX_DEV = 768
ROWS = 8
PACKED = 24576
OWNED = 49152
N_DP = 8
N_CONTEXT = 32


def route_plan(key):
    bucket = 2 * CTX_DEV // N_DP
    spare_count = CTX_DEV - bucket
    other_slots = (N_DP - 1) * bucket
    row_ids = jnp.arange(N_DP, dtype=jnp.int32)
    shard_ids = jnp.arange(N_CONTEXT, dtype=jnp.int32)
    full_owner = (row_ids[None, :] + shard_ids[:, None]) % N_DP
    scores = jax.random.randint(key, (N_CONTEXT, N_DP, other_slots), 0, 1 << 19) * other_slots
    scores = scores + jnp.arange(other_slots, dtype=jnp.int32)[None, None, :]
    sorted_idx = jnp.argsort(scores, axis=2)
    rank_of = jnp.argsort(sorted_idx, axis=2)
    chosen = (rank_of < spare_count).astype(jnp.int32).reshape(N_CONTEXT, N_DP, N_DP - 1, bucket)
    extra_count = jnp.sum(chosen, axis=3)
    counts = jnp.concatenate([jnp.full((N_CONTEXT, N_DP, 1), bucket, jnp.int32), extra_count], axis=2)
    order_owner = (full_owner[:, :, None] + row_ids[None, None, :]) % N_DP
    upper_end = jnp.cumsum(counts, axis=2)
    lower_end = upper_end - counts
    token_ids = jnp.arange(CTX_DEV, dtype=jnp.int32)[None, None, None, :]
    inside = (token_ids >= lower_end[..., None]) & (token_ids < upper_end[..., None])
    pack_table = jnp.sum(jnp.where(inside, order_owner[..., None] * bucket + token_ids - lower_end[..., None], 0), axis=2)
    pack_table = pack_table.transpose(1, 0, 2).reshape(N_DP, N_CONTEXT * CTX_DEV).astype(jnp.int32)
    per_owner = jnp.sum(counts[..., None] * (order_owner[..., None] == row_ids[None, None, None, :]).astype(jnp.int32), axis=2)
    flow_counts = per_owner.transpose(0, 2, 1)
    top_end = jnp.cumsum(flow_counts, axis=2)
    base_end = top_end - flow_counts
    owner_places = jnp.arange(2 * CTX_DEV, dtype=jnp.int32)[None, None, None, :]
    inside_owner = (owner_places >= base_end[..., None]) & (owner_places < top_end[..., None])
    send_table = jnp.sum(jnp.where(inside_owner, row_ids[None, None, :, None] * bucket + owner_places - base_end[..., None], 0), axis=2)
    filled = jnp.any(inside_owner, axis=2)
    send_table = jnp.where(filled, send_table, -1)
    send_table = send_table.transpose(1, 0, 2).reshape(N_DP, N_CONTEXT * 2 * CTX_DEV).astype(jnp.int32)
    return (send_table, pack_table)


def episode_plan(key):
    key = jax.random.fold_in(key, 91)
    row_length = CTX_DEV * N_CONTEXT
    token_ids = jnp.arange(row_length, dtype=jnp.int32)
    start_marks = jax.random.randint(key, (N_DP, row_length), 0, 2 * CTX_DEV) == 0
    row_ids = jnp.arange(N_DP, dtype=jnp.int32)[:, None]
    begins = start_marks & (row_ids > 0) | (token_ids[None, :] == 0)
    first_spot = lax.cummax(jnp.where(begins, token_ids[None, :], 0), axis=1)
    next_start = jnp.concatenate([jnp.where(begins[:, 1:], token_ids[None, 1:], row_length), jnp.full((N_DP, 1), row_length, jnp.int32)], axis=1)
    finish_spot = lax.cummin(next_start, axis=1, reverse=True)
    return ((token_ids[None, :] - first_spot).astype(jnp.int32), (finish_spot - first_spot).astype(jnp.int32))


def draw_send_slot(key, part):
    shared = route_plan(key)
    return shared[0]


def draw_pack_slot(key, part):
    shared = route_plan(key)
    return shared[1]


def draw_positions(key, part):
    shared = episode_plan(key)
    return shared[0]


def draw_episode_len(key, part):
    shared = episode_plan(key)
    return shared[1]


def levels(rng, dims, pieces, low, top_value):
    gain = 1.0
    for dim, blocks in pieces:
        steps = jax.random.uniform(jax.random.fold_in(jax.random.fold_in(rng, 6), dim), (blocks,), jnp.float32, low / len(pieces), top_value / len(pieces))
        gain = gain * jnp.repeat(jnp.exp(steps), dims[dim] // blocks).reshape((-1,) + (1,) * (len(dims) - 1 - dim))
    return gain


def scatter_about(key, shape, width, most, cuts=(), kind=jnp.bfloat16):
    gain = levels(key, shape, cuts, -0.22, 0.18) if cuts else 1.0
    values = jax.random.normal(key, shape, jnp.float32) * width * gain
    return jnp.minimum(jnp.maximum(values, -most), most).astype(kind)


def setup_inputs(seed: int = 0) -> dict:
    streams_of = jax.random.split(jax.random.key(seed), 11)
    hidden = scatter_about(streams_of[0], (ROWS, PACKED, D), 1.0, 6.0, ((0, 8), (1, 32)))
    norm_gain = jnp.clip(1.0 + 0.18 * jax.random.normal(streams_of[1], (D,), jnp.float32), 0.099609375, 1.8984375).astype(jnp.bfloat16)
    w_in = scatter_about(streams_of[2], (D, VH), D ** -0.5, 0.0625, ((0, 32),))
    w_out = scatter_about(streams_of[3], (VH,), VH ** -0.5, 0.25)
    rewards = scatter_about(streams_of[4], (ROWS, OWNED), 0.02, 0.3125, ((0, 8), (1, 32)), jnp.float32)
    old_values = scatter_about(streams_of[5], (ROWS, OWNED), 0.6, 6.0, ((0, 8), (1, 32)), jnp.float32)
    send_slot = draw_send_slot(jax.random.fold_in(streams_of[10], 71), 0)
    pack_slot = draw_pack_slot(jax.random.fold_in(streams_of[10], 71), 0)
    positions = draw_positions(jax.random.fold_in(streams_of[10], 71), 0)
    episode_len = draw_episode_len(jax.random.fold_in(streams_of[10], 71), 0)
    return {"hidden": hidden, "norm_gain": norm_gain, "w_in": w_in, "w_out": w_out, "rewards": rewards, "old_values": old_values, "send_slot": send_slot, "pack_slot": pack_slot, "positions": positions, "episode_len": episode_len}


def head_block(token_rows, norm_gain, w_in, w_out):
    widened = token_rows.astype(jnp.float32)
    inv_rms = lax.rsqrt(lax.optimization_barrier(jnp.mean(widened * widened, axis=1, keepdims=True)) + 1e-05)
    normed = (widened * inv_rms * norm_gain.astype(jnp.float32)[None, :]).astype(jnp.bfloat16)
    pre_act = jnp.dot(normed, w_in, preferred_element_type=jnp.float32)
    activated = jax.nn.silu(pre_act).astype(jnp.bfloat16)
    return jnp.dot(activated, w_out, preferred_element_type=jnp.float32)

def reference(hidden, norm_gain, w_in, w_out, rewards, old_values, send_slot, pack_slot, positions, episode_len):
    row_length = CTX_DEV * N_CONTEXT
    bucket = 2 * CTX_DEV // N_DP
    own_slots = 2 * CTX_DEV
    token_blocks = hidden.reshape(N_DP * N_CONTEXT, CTX_DEV, D)
    values = lax.map(lambda token_rows: head_block(token_rows, norm_gain, w_in, w_out), token_blocks)
    values = values.reshape(N_DP, row_length)
    owner_slots = send_slot.reshape(N_DP, N_CONTEXT, own_slots)
    target = jnp.where(owner_slots < 0, N_DP * bucket, owner_slots).astype(jnp.int32)
    source = jnp.stack([rewards, old_values]).reshape(2, N_DP, N_CONTEXT, own_slots)
    owner_idx = jnp.arange(N_DP, dtype=jnp.int32)[:, None, None]
    shard_idx = jnp.arange(N_CONTEXT, dtype=jnp.int32)[None, :, None]
    buckets = jnp.zeros((2, N_DP, N_CONTEXT, N_DP * bucket), jnp.float32)
    buckets = buckets.at[:, owner_idx, shard_idx, target].set(source, mode='drop')
    packed_slots = pack_slot.reshape(N_DP, N_CONTEXT, CTX_DEV).astype(jnp.int32)
    row_idx = jnp.arange(N_DP, dtype=jnp.int32)[:, None, None]
    senders = packed_slots // bucket
    picked = buckets[:, senders, shard_idx, row_idx * bucket + packed_slots % bucket]
    reward_row = picked[0].reshape(N_DP, row_length)
    old_row = picked[1].reshape(N_DP, row_length)
    keep_mask = jnp.where(positions == 0, 0.0, 1.0).astype(jnp.float32)
    len_float = episode_len.astype(jnp.float32)
    decay = len_float / (len_float + 20.0)

    def backward(carried, column):
        adv_in, ret_in = carried
        reward, value_t, keep_t, decay_t = column
        advantage = reward - value_t + adv_in
        return_t = reward + ret_in
        return ((keep_t * (value_t + decay_t * advantage), keep_t * return_t), (advantage, return_t))
    zero_rows = jnp.zeros((N_DP,), jnp.float32)
    _, (adv_cols, ret_cols) = lax.scan(backward, (zero_rows, zero_rows), (reward_row.T, values.T, keep_mask.T, decay.T), reverse=True)
    advantages = adv_cols.T
    returns = ret_cols.T
    clipped = old_row + jnp.clip(values - old_row, -0.2, 0.2)
    value_loss = 0.5 * jnp.maximum(jnp.square(values - returns), jnp.square(clipped - returns))
    result = jnp.stack([advantages, value_loss]).reshape(2, N_DP, N_CONTEXT, CTX_DEV)
    returned = jnp.zeros((2, N_DP, N_CONTEXT, N_DP * bucket), jnp.float32)
    returned = returned.at[:, row_idx, shard_idx, packed_slots].set(result)
    safe_slots = jnp.where(owner_slots < 0, 0, owner_slots).astype(jnp.int32)
    fetched = returned[:, safe_slots // bucket, shard_idx, owner_idx * bucket + safe_slots % bucket]
    fetched = jnp.where(owner_slots[None] < 0, 0.0, fetched)
    return (fetched[0].reshape(N_DP, N_CONTEXT * own_slots), fetched[1].reshape(N_DP, N_CONTEXT * own_slots))
```

```python
import jax
import jax.numpy as jnp
from jax import lax
from jax.experimental import pallas as pl
from jax.experimental.pallas import tpu as pltpu
from jax.sharding import PartitionSpec as P

F32 = jnp.float32
BF16 = jnp.bfloat16
MESH = pl.DeviceIdType.MESH

NX, NY, NZ = 4, 4, 8
NDP = 2 * NX
T = 768
S = 1536
D = 8192
VH = 512
KB = 256
BUCKET = 192
BW = 256
GB = 4
NG = 8
KG = GB * KB
EPS = 1e-05

HALF = KB // 2
XR = 48
TREE = HALF - XR

BLOCKS = [
    (0, 0), (-1, 0), (0, 1), (0, -1), (1, 0), (0, 2), (0, -2), (1, 1),
    (-1, 1), (1, -2), (-1, -2), (1, -1), (0, -3), (-1, -1), (1, 2), (2, 0),
    (-1, 2), (0, 3), (2, 2), (2, -2), (2, 1), (-1, -3), (1, -3), (2, -1),
    (0, 4), (1, 4), (1, 3), (-1, 3), (2, -3), (-1, 4), (2, 4), (2, 3),
]
GROUPS = [BLOCKS[GB * g : GB * g + GB] for g in range(NG)]
SLOT = {b: i for i, b in enumerate(BLOCKS)}
PARTS = [(GB * g, GB * g + GB) for g in range(NG - 1)] + [(28, 30), (30, 32)]

PLAN = [
    ('load', 0),
    ('load', 1),
    ('load', 2),
    ('load', 3),
    ('load', 4),
    ('load', 5),
    ('load', 6),
    ('load', 7),
    ('to_rows',),
    ('coefficients',),
    ('pack_table',),
    ('tails',),
    ((4,), ()),
    ((1, 2, 3), ()),
    ((65, 66, 67), ()),
    ('squares', 0, 0),
    ('squares', 0, 1),
    ((), (1,)),
    ((), (65,)),
    ((68,), ()),
    ((15,), ()),
    ('squares', 1, 0),
    ('squares', 1, 1),
    ((), (5,)),
    ((), (6, 2, 3)),
    ((79,), ()),
    ('squares', 2, 0),
    ((), (4,)),
    ('squares', 2, 1),
    ((), (68,)),
    ((), (66, 67)),
    ((), (69, 70)),
    ((7,), ()),
    ((11,), ()),
    ('squares', 3, 0),
    ('squares', 3, 1),
    ((36, 8, 13), ()),
    ('at_rows',),
    ((33, 5, 6), ()),
    ((72, 77), ()),
    ('returns_scan',),
    ((34, 69, 70), ()),
    ((35, 71, 75), ()),
    ('squares', 4, 0),
    ('squares', 4, 1),
    ((47, 20, 23), ()),
    ('squares', 5, 0),
    ((), (33,)),
    ('squares', 5, 1),
    ('squares', 6, 0),
    ((87,), (14, 16)),
    ('squares', 6, 1),
    ((), (9,)),
    ((), (37, 10)),
    ((), (7,)),
    ((), (38, 8, 12)),
    ((), (11,)),
    ((), (34, 13)),
    ((), (76,)),
    ((), (72,)),
    ('squares', 7, 0),
    ((), (35, 15, 24, 17, 77)),
    ((), (79, 80)),
    ((), (36,)),
    ((), (71,)),
    ('squares', 7, 1),
    ((39,), (74, 75)),
    ('inverse',),
    ((9, 84), (78, 81)),
    ((43,), (88,)),
    ((), (73,)),
    ((10,), ()),
    ((40,), ()),
    ((12,), ()),
    ((74,), ()),
    ((45,), ()),
    ((14,), ()),
    ((76,), ()),
    ((), (46,)),
    ((), (18,)),
    ((), (19,)),
    ((37,), ()),
    ((73,), ()),
    ((16,), ()),
    ((), (48,)),
    ((), (20,)),
    ((), (21,)),
    ((38,), ()),
    ((19,), ()),
    ((17,), ()),
    ('matmul', 0, 0),
    ((52, 83, 80, 81), (41, 22, 23, 86)),
    ((55,), (42, 85)),
    ('carry_z',),
    ((78,), ()),
    ((22,), ()),
    ('matmul', 0, 1),
    ((41, 18, 21), (39, 25, 29)),
    ((82,), (26,)),
    ((), (40, 27)),
    ('tails_in',),
    ((42, 85), (44, 84, 87)),
    ((), (82,)),
    ((), (83,)),
    ((), (90,)),
    ((), (43, 91)),
    ((26,), ()),
    ((44,), ()),
    ((86,), ()),
    ((), (89,)),
    ((), (93,)),
    ((27,), ()),
    ((46,), ()),
    ((), (45,)),
    ((28,), ()),
    ((24,), ()),
    ((48,), ()),
    ((), (28,)),
    ((), (47,)),
    ((92,), ()),
    ((51, 91), ()),
    ('matmul', 1, 0),
    ((49, 88, 25, 90), (56, 92)),
    ('matmul', 1, 1),
    ((54, 31, 29), (49,)),
    ((95,), ()),
    ((93,), ()),
    ((50,), ()),
    ('matmul', 2, 0),
    ((53, 89), (50, 30, 31)),
    ('matmul', 2, 1),
    ((58, 30), (51, 95)),
    ((), (52,)),
    ('matmul', 3, 0),
    ((59, 94), (53, 94)),
    ((60,), ()),
    ('matmul', 3, 1),
    ((56,), (54,)),
    ('returns_done',),
    ((), (55,)),
    ((), (57,)),
    ((), (61,)),
    ((57,), ()),
    ((), (58,)),
    ((63,), ()),
    ('matmul', 4, 0),
    ('matmul', 4, 1),
    ((61,), (59,)),
    ((), (60,)),
    ((), (62,)),
    ((62,), ()),
    ('matmul', 5, 0),
    ('matmul', 5, 1),
    ((), (63,)),
    ('matmul', 6, 0),
    ('matmul', 6, 1),
    ('matmul', 7, 0),
    ('matmul', 7, 1),
    ('matmul', 8, 0),
    ('matmul', 8, 1),
]


def children_yz(dy, dz):
    out = []
    if dz == 0 and dy == 0:
        out += [((1, 0), 1), ((-1, 0), 1), ((1, 0), 2)]
    if dz in (0, 1, 2) or (dz == 3 and dy == 0):
        out += [((0, 1), 1)]
    if dz in (0, -1, -2) or (dz == -3 and dy != 0):
        out += [((0, -1), 1)]
    return out


def children_zy(dy, dz):
    out = []
    if dy == 0:
        if dz == 0:
            out += [((0, 1), 2), ((0, -1), 2), ((0, 1), 1), ((0, -1), 1)]
        elif dz == 2:
            out += [((0, 1), 2), ((0, 1), 1)]
        elif dz == -2:
            out += [((0, -1), 1)]
        out += [((1, 0), 1), ((-1, 0), 1)]
    elif dy == 1 and dz in (0, 1, 2, 3):
        out += [((1, 0), 1)]
    elif dy == -1 and dz in (-1, -2, -3, 4):
        out += [((-1, 0), 1)]
    return out


def after(b, step, hops):
    dy, dz = b[0] + step[0] * hops, b[1] + step[1] * hops
    return (2 if dy == -2 else dy, 4 if dz == -4 else dz)


def split3(v):
    hi = v.astype(BF16).astype(F32)
    rest = v - hi
    mid = rest.astype(BF16).astype(F32)
    return hi, mid, rest - mid


def rows_of(parts, width):
    row = lax.broadcasted_iota(jnp.int32, (8, width), 0)
    out = jnp.zeros((8, width), F32)
    for i, part in enumerate(parts):
        out = jnp.where(row == i, jnp.broadcast_to(part, (8, width)), out)
    return out


def quotient(s):
    q = jnp.zeros_like(s)
    for i in range(1, NDP):
        q = q + (s >= BUCKET * i).astype(jnp.int32)
    return q


def spread(parts, q):
    return jnp.concatenate(
        [jnp.where(q == r, parts, 0.0) for r in range(NDP)], axis=0
    ).astype(BF16)


def collect(table, q):
    out = jnp.where(q == 0, table[0:8], 0.0)
    for r in range(1, NDP):
        out = out + jnp.where(q == r, table[8 * r : 8 * r + 8], 0.0)
    return out


def nt_dot(a, b):
    return lax.dot_general(a, b, (((1,), (1,)), ((), ())), preferred_element_type=F32)


def kernel(
    hid_hbm, gain_hbm, win_hbm, wout_hbm, rew_hbm, old_hbm, send_hbm, pack_hbm, pos_hbm, len_hbm,
    adv_out, loss_out,
    hid, wall, acc, ssq, inv, gain_in, win, wout, rew, old, send, pack, pos, elen,
    hot_send, hot_pack, osend, oland, rsend, rland, lev, tail_a, rowdat,
    ysend, yland, zsend, zland, ysend2, yland2, zsend2, zland2, tsend, tland, isend, iland, own,
    sem_hid, sem_small, tree_recv, rest_recv, x_recv, sib_recv, sem_sent, sem_ex,
):
    dp = lax.axis_index("dp")
    ctx = lax.axis_index("context")
    y = lax.rem(ctx, NY)
    z = lax.div(ctx, NY)
    core = lax.rem(dp, 2)
    even = 1 - lax.rem(lax.div(dp, 2), 2)

    def ctx_at(dy, dz):
        return lax.rem(z + dz + NZ, NZ) * NY + lax.rem(y + dy + NY, NY)

    def dp_at(step):
        return lax.rem(dp + step + NDP, NDP)

    sibling = dp + 1 - 2 * core

    def at(dy, dz):
        return (dp, ctx_at(dy, dz))

    smalls = [
        (send_hbm, send), (rew_hbm, rew), (old_hbm, old), (pack_hbm, pack),
        (gain_hbm, gain_in), (pos_hbm, pos), (len_hbm, elen), (wout_hbm, wout), (win_hbm, win),
    ]
    small_copies = [
        pltpu.make_async_copy(src, dst, sem_small.at[i]) for i, (src, dst) in enumerate(smalls)
    ]
    small_copies[8].start()
    small_copies[4].start()

    peers = [at(k, 0) for k in range(1, NY)] + [at(0, k) for k in range(1, NZ)]
    peers += [(dp_at(k), ctx) for k in range(1, NDP)]
    barrier = pltpu.get_barrier_semaphore()
    for peer in peers:
        pl.semaphore_signal(barrier, inc=1, device_id=peer, device_id_type=MESH)
    for i in (0, 1, 2, 3, 5, 6, 7):
        small_copies[i].start()

    small_copies[4].wait()
    small_copies[8].wait()
    square = (KB, KB)
    diagonal = lax.broadcasted_iota(jnp.int32, square, 0) == lax.broadcasted_iota(
        jnp.int32, square, 1
    )
    gains = jnp.broadcast_to(gain_in[...].astype(F32).reshape(1, KB), square)
    wall[0] = jnp.dot(
        jnp.where(diagonal, gains, 0.0).astype(BF16), win[...], preferred_element_type=F32
    ).astype(BF16)

    def load(g):
        for j in range(GB):
            b = GROUPS[g][j]
            column = pl.multiple_of(ctx_at(-b[0], -b[1]) * KB, KB)
            pltpu.make_async_copy(
                hid_hbm.at[0, :, pl.ds(column, KB)], hid.at[g, :, pl.ds(j * KB, KB)], sem_hid.at[g]
            ).start()

    pl.semaphore_wait(barrier, len(peers))

    base = HALF * core
    rest_rows = pl.ds(pl.multiple_of(base + XR, 16), TREE - XR)
    x_rows = pl.ds(pl.multiple_of(base + TREE * even, 16), XR)
    x_lands = pl.ds(pl.multiple_of(base + TREE * (1 - even), 16), XR)
    half_rows = pl.ds(pl.multiple_of(base, 16), HALF)
    other_rows = pl.ds(pl.multiple_of(HALF - base, 16), HALF)
    x_peer = (dp_at(2 - 4 * core), ctx)

    def tree_step(c, b, first):
        slot = SLOT[b]
        rows = x_rows if first else rest_rows
        arrived = tree_recv if first else rest_recv
        if slot:
            here = wall.at[slot, rows]
            pltpu.make_async_copy(here, here, arrived.at[slot]).wait()
        for step, hops in (children_yz if c == 0 else children_zy)(*b):
            to = SLOT[after(b, step, hops)]
            pltpu.make_async_remote_copy(
                src_ref=wall.at[slot, rows],
                dst_ref=wall.at[to, rows],
                send_sem=sem_sent.at[0],
                recv_sem=arrived.at[to],
                device_id=at(step[0] * hops, step[1] * hops),
                device_id_type=MESH,
            ).start()
        if slot and first:
            part = wall.at[slot, x_rows]
            pltpu.make_async_remote_copy(
                src_ref=part,
                dst_ref=part,
                send_sem=sem_sent.at[1],
                recv_sem=x_recv.at[slot],
                device_id=x_peer,
                device_id_type=MESH,
            ).start()

    def x_step(slot):
        part = wall.at[slot, x_lands]
        pltpu.make_async_copy(part, part, x_recv.at[slot]).wait()

    def hand_over(slot):
        part = wall.at[slot, half_rows]
        pltpu.make_async_remote_copy(
            src_ref=part,
            dst_ref=part,
            send_sem=sem_sent.at[2],
            recv_sem=sib_recv.at[slot],
            device_id=(sibling, ctx),
            device_id_type=MESH,
        ).start()

    def handed(slot):
        part = wall.at[slot, other_rows]
        pltpu.make_async_copy(part, part, sib_recv.at[slot]).wait()

    seen = [set(), set()]

    def arrivals(c, codes):
        for code in codes:
            slot = code % 32
            if code // 32 == 1:
                x_step(slot)
            else:
                tree_step(c, BLOCKS[slot], code < 32)
            seen[c].add(code)
            if {slot, slot + 32, slot + 64} <= seen[c]:
                hand_over(slot)

    def by_core(first, second):
        if first:

            @pl.when(core == 0)
            def _():
                arrivals(0, first)

        if second:

            @pl.when(core == 1)
            def _():
                arrivals(1, second)

    def exchange(pairs, send_sem, recv_sem):
        for src, dst, device in pairs:
            pltpu.make_async_remote_copy(
                src_ref=src, dst_ref=dst, send_sem=send_sem, recv_sem=recv_sem,
                device_id=device, device_id_type=MESH,
            ).start()

    def await_bytes(ref, sem):
        pltpu.make_async_copy(ref, ref, sem).wait()

    def along_y(src, dst, sem):
        exchange([(src, dst, at(k, 0)) for k in range(1, NY)], sem_ex.at[sem], sem_ex.at[sem + 1])

    def along_z(src, dst, sem):
        exchange([(src, dst, at(0, k)) for k in range(1, NZ)], sem_ex.at[sem], sem_ex.at[sem + 1])

    def along_dp(src, dst, sem):
        exchange(
            [(src.at[dp_at(k)], dst, (dp_at(k), ctx)) for k in range(1, NDP)],
            sem_ex.at[sem],
            sem_ex.at[sem + 1],
        )

    def to_rows():
        for i in range(3):
            small_copies[i].wait()
        s = send[...]
        q = quotient(s)
        k = s - BUCKET * q
        hot_send[...] = (
            lax.broadcasted_iota(jnp.int32, (BW, S), 0) == jnp.broadcast_to(k, (BW, S))
        ).astype(F32).astype(BF16)
        parts = rows_of(split3(rew[...]) + split3(old[...]), S)
        table = nt_dot(spread(parts, q), hot_send[...])
        for r in range(NDP):
            osend[r] = table[8 * r : 8 * r + 8]
        along_dp(osend, oland.at[dp], 4)
        oland[pl.ds(dp, 1)] = osend[pl.ds(dp, 1)]

    def pack_table():
        small_copies[3].wait()
        s = pack[...]
        k = s - BUCKET * quotient(s)
        hot_pack[...] = (
            lax.broadcasted_iota(jnp.int32, (BW, T), 0) == jnp.broadcast_to(k, (BW, T))
        ).astype(F32).astype(BF16)

    def at_rows():
        await_bytes(oland.at[pl.ds(0, NDP - 1)], sem_ex.at[5])
        table = oland[...].reshape(8 * NDP, BW).astype(BF16)
        got = collect(
            jnp.dot(table, hot_pack[...], preferred_element_type=F32), quotient(pack[...])
        )
        rowdat[0] = jnp.broadcast_to(got[0:1] + got[1:2] + got[2:3], (8, T))
        rowdat[1] = jnp.broadcast_to(got[3:4] + got[4:5] + got[5:6], (8, T))

    lane = lax.broadcasted_iota(jnp.int32, (8, T), 1)
    row8 = lax.broadcasted_iota(jnp.int32, (8, T), 0)
    strides = [(1, 3), (4, 3), (16, 3), (64, 3), (256, 2)]

    def later(v, d, fill):
        return jnp.where(lane < T - d, pltpu.roll(v, T - d, 1), fill)

    def wide(slab):
        return jnp.concatenate([slab] * (T // 128), axis=1)

    def slab_of(v):
        return jnp.broadcast_to(v[:, 0:1], (8, 128))

    def coefficients():
        small_copies[5].wait()
        small_copies[6].wait()
        keep = jnp.where(pos[...] == 0, 0.0, 1.0).astype(F32)
        below = elen[...].astype(F32) + 20.0
        lost = 20.0 / below
        lost = lost + lost * (20.0 - lost * below) * 0.05
        keep8 = jnp.broadcast_to(keep, (8, T))
        lost8 = jnp.broadcast_to(lost, (8, T))
        rowdat[2] = keep8
        rowdat[3] = lost8
        a = jnp.where(row8 == 1, keep8, keep8 * (1.0 - lost8))
        i = 0
        for d, count in strides:
            reach = a
            for k in range(1, count + 1):
                lev[i] = jnp.where(lane < T - k * d, reach, 0.0)
                reach = reach * later(a, k * d, 1.0)
                i += 1
            a = reach
        tail_a[...] = later(a, 1, 1.0)
        ysend[0] = slab_of(a)

    def scan(b):
        i = 0
        for d, count in strides:
            total = b
            for k in range(1, count + 1):
                total = total + lev[i] * pltpu.roll(b, T - k * d, 1)
                i += 1
            b = total
        return b

    def tails():
        table = nt_dot(
            spread(rows_of(split3(tail_a[0:1]), T), quotient(pack[...])), hot_pack[...]
        )
        for r in range(NDP):
            tsend[r] = table[8 * r : 8 * r + 8]
        along_dp(tsend, tland.at[dp], 16)
        tland[pl.ds(dp, 1)] = tsend[pl.ds(dp, 1)]

    def to_owner(land):
        table = land[...].reshape(8 * NDP, BW).astype(BF16)
        return collect(
            jnp.dot(table, hot_send[...], preferred_element_type=F32), quotient(send[...])
        )

    def tails_in():
        await_bytes(tland.at[pl.ds(0, NDP - 1)], sem_ex.at[17])
        got = to_owner(tland)
        own[0:1] = got[0:1] + got[1:2] + got[2:3]

    def returns_scan():
        b = scan(jnp.where(row8 == 1, rowdat[2] * rowdat[0], 0.0))
        rowdat[4] = later(b, 1, 0.0)
        ysend[1] = slab_of(b)
        yland[pl.ds(y, 1)] = ysend[...][None]
        along_y(ysend, yland.at[y], 6)

    def compose(parts, here, count, land):
        one = jnp.ones((8, 128), F32)
        zero = jnp.zeros((8, 128), F32)
        a, b, sa, sb = one, zero, one, zero
        for i in reversed(range(count)):
            ai, bi = land(i)
            b = bi + ai * b
            a = ai * a
            after = i > here
            sb = jnp.where(after, bi + ai * sb, sb)
            sa = jnp.where(after, ai * sa, sa)
        return a, b, sa, sb

    def carry_z():
        await_bytes(yland.at[pl.ds(0, NY - 1)], sem_ex.at[7])
        a, b, _, _ = compose(None, y, NY, lambda i: (yland[i, 0], yland[i, 1]))
        zsend[0] = a
        zsend[1] = b
        zland[pl.ds(z, 1)] = zsend[...][None]
        along_z(zsend, zland.at[z], 8)

    def returns_done():
        await_bytes(zland.at[pl.ds(0, NZ - 1)], sem_ex.at[9])
        _, _, _, inflow = compose(None, z, NZ, lambda i: (zland[i, 0], zland[i, 1]))
        _, _, sa, sb = compose(None, y, NY, lambda i: (yland[i, 0], yland[i, 1]))
        inflow = sa * inflow + sb
        carried = tail_a[...] * wide(inflow) + rowdat[4]
        ret = rowdat[0] + carried
        rowdat[5] = jnp.broadcast_to(ret[1:2], (8, T))
        keep8, lost8 = rowdat[2], rowdat[3]
        rowdat[6] = keep8 * (1.0 - lost8) * rowdat[0]
        rowdat[7] = keep8 * lost8

    TR = 32

    def over_rows(body, half):
        def one(i, _):
            body(pl.ds(pl.multiple_of(half * (T // 2) + i * TR, TR), TR))
            return 0

        lax.fori_loop(0, T // 2 // TR, one, 0)

    def squares(g, half):
        if half == 0:
            pltpu.make_async_copy(hid.at[g], hid.at[g], sem_hid.at[g]).wait()

        def body(rows):
            v = hid[g, rows, :].astype(F32)
            v = v * v
            total = v[:, 0:128]
            for j in range(1, KG // 128):
                total = total + v[:, 128 * j : 128 * j + 128]
            ssq[rows, :] = total if g == 0 else ssq[rows, :] + total

        over_rows(body, half)

    def inverse():
        def body(i, _):
            rows = pl.ds(pl.multiple_of(i * 128, 128), 128)
            mean = jnp.sum(ssq[rows, :], axis=1, keepdims=True) * (1.0 / D)
            inv[rows, :] = jnp.broadcast_to(lax.rsqrt(mean + EPS), (128, 128))
            return 0

        lax.fori_loop(0, T // 128, body, 0)

    def matmul(part, half):
        first, end = PARTS[part]
        if half == 0:
            for slot in range(first, end):
                if slot:
                    handed(slot)
        cols = slice(256 * half, 256 * half + 256)
        w = wall[first:end, :, cols].reshape(KB * (end - first), 256)
        g, offset = divmod(first * KB, KG)
        v = jnp.dot(
            hid[g, :, offset : offset + KB * (end - first)], w, preferred_element_type=F32
        )
        acc[:, cols] = v if part == 0 else acc[:, cols] + v

    items = dict(
        load=load, to_rows=to_rows, coefficients=coefficients, tails=tails,
        pack_table=pack_table, at_rows=at_rows, returns_scan=returns_scan, carry_z=carry_z,
        returns_done=returns_done, squares=squares, inverse=inverse,
        matmul=matmul, tails_in=tails_in,
    )
    for c in range(2):

        @pl.when(core == c)
        def _(c=c):
            tree_step(c, (0, 0), True)
            tree_step(c, (0, 0), False)

    for step in PLAN:
        if isinstance(step[0], str):
            items[step[0]](*step[1:])
        else:
            by_core(*step)

    for i in (7,):
        small_copies[i].wait()
    w_row = jnp.broadcast_to(wout[...].astype(F32).reshape(1, VH), (16, VH)).astype(BF16)

    def activate(i, _):
        rows = pl.ds(pl.multiple_of(i * 128, 128), 128)
        half = acc[rows, :] * jnp.concatenate([inv[rows, :] * 0.5] * (VH // 128), axis=1)
        act = (half * jnp.tanh(half) + half).astype(BF16)
        hid[0, rows, 0:VH] = act
        return 0

    lax.fori_loop(0, T // 128, activate, 0)
    values = nt_dot(w_row, hid[0, :, 0:VH])[0:8]

    b = scan(rowdat[7] * values + rowdat[6])
    slab = slab_of(b)
    ysend2[...] = slab
    yland2[pl.ds(y, 1)] = slab[None]
    along_y(ysend2, yland2.at[y], 10)
    base_adv = rowdat[0] - values + later(b, 1, 0.0)
    old_row, ret = rowdat[1], rowdat[5]
    clipped = old_row + jnp.clip(values - old_row, -0.2, 0.2)
    loss = 0.5 * jnp.maximum(jnp.square(values - ret), jnp.square(clipped - ret))
    parts = rows_of(split3(base_adv[0:1]) + split3(loss[0:1]), T)
    table = nt_dot(spread(parts, quotient(pack[...])), hot_pack[...])
    for r in range(NDP):
        rsend[r] = table[8 * r : 8 * r + 8]
    along_dp(rsend, rland.at[dp], 14)
    rland[pl.ds(dp, 1)] = rsend[pl.ds(dp, 1)]

    await_bytes(yland2.at[pl.ds(0, NY - 1)], sem_ex.at[11])
    _, b, sa, sb = compose(None, y, NY, lambda i: (yland[i, 0], yland2[i]))
    zsend2[...] = b
    zland2[pl.ds(z, 1)] = b[None]
    along_z(zsend2, zland2.at[z], 12)
    await_bytes(rland.at[pl.ds(0, NDP - 1)], sem_ex.at[15])
    got = to_owner(rland)
    own[1:2] = got[0:1] + got[1:2] + got[2:3]
    old[...] = got[3:4] + got[4:5] + got[5:6]
    loss_copy = pltpu.make_async_copy(old, loss_out, sem_small.at[1])
    loss_copy.start()
    q = quotient(send[...])
    await_bytes(zland2.at[pl.ds(0, NZ - 1)], sem_ex.at[13])
    _, _, _, inflow = compose(None, z, NZ, lambda i: (zland[i, 0], zland2[i]))
    inflow = sa * inflow + sb
    isend[...] = inflow
    iland[pl.ds(dp, 1)] = inflow[None]
    exchange(
        [(isend, iland.at[dp], (dp_at(k), ctx)) for k in range(1, NDP)], sem_ex.at[18], sem_ex.at[19]
    )

    await_bytes(wall.at[pl.ds(0, 31), pl.ds(0, TREE)], sem_sent.at[0])
    await_bytes(wall.at[pl.ds(0, 31), pl.ds(0, XR)], sem_sent.at[1])
    await_bytes(wall.at[pl.ds(0, 31), pl.ds(0, HALF)], sem_sent.at[2])
    await_bytes(oland.at[pl.ds(0, NDP - 1)], sem_ex.at[4])
    await_bytes(yland.at[pl.ds(0, NY - 1)], sem_ex.at[6])
    await_bytes(zland.at[pl.ds(0, NZ - 1)], sem_ex.at[8])
    await_bytes(yland2.at[pl.ds(0, NY - 1)], sem_ex.at[10])
    await_bytes(zland2.at[pl.ds(0, NZ - 1)], sem_ex.at[12])
    await_bytes(rland.at[pl.ds(0, NDP - 1)], sem_ex.at[14])
    await_bytes(tland.at[pl.ds(0, NDP - 1)], sem_ex.at[16])

    await_bytes(iland.at[pl.ds(0, NDP - 1)], sem_ex.at[19])
    flow = jnp.zeros((1, S), F32)
    for r in range(NDP):
        here = jnp.concatenate([iland[r, 0:1]] * (S // 128), axis=1)
        flow = flow + jnp.where(q == r, here, 0.0)
    rew[...] = own[1:2] + own[0:1] * flow
    adv_copy = pltpu.make_async_copy(rew, adv_out, sem_small.at[0])
    adv_copy.start()
    await_bytes(iland.at[pl.ds(0, NDP - 1)], sem_ex.at[18])
    loss_copy.wait()
    adv_copy.wait()


def local(
    hidden, norm_gain, w_in, w_out, rewards, old_values, send_slot, pack_slot, positions, episode_len
):
    outside = pl.BlockSpec(memory_space=pltpu.HBM)
    vmem = pltpu.VMEM
    dma = pltpu.SemaphoreType.DMA
    return pl.pallas_call(
        kernel,
        out_shape=(jax.ShapeDtypeStruct((1, S), F32), jax.ShapeDtypeStruct((1, S), F32)),
        in_specs=[outside] * 10,
        out_specs=(outside, outside),
        scratch_shapes=[
            vmem((NG, T, KG), BF16),
            vmem((NY * NZ, KB, VH), BF16),
            vmem((T, VH), F32),
            vmem((T, 128), F32),
            vmem((T, 128), F32),
            vmem((KB,), BF16),
            vmem((KB, VH), BF16),
            vmem((VH,), BF16),
            vmem((1, S), F32),
            vmem((1, S), F32),
            vmem((1, S), jnp.int32),
            vmem((1, T), jnp.int32),
            vmem((1, T), jnp.int32),
            vmem((1, T), jnp.int32),
            vmem((BW, S), BF16),
            vmem((BW, T), BF16),
            vmem((NDP, 8, BW), F32),
            vmem((NDP, 8, BW), F32),
            vmem((NDP, 8, BW), F32),
            vmem((NDP, 8, BW), F32),
            vmem((14, 8, T), F32),
            vmem((8, T), F32),
            vmem((8, 8, T), F32),
            vmem((2, 8, 128), F32),
            vmem((NY, 2, 8, 128), F32),
            vmem((2, 8, 128), F32),
            vmem((NZ, 2, 8, 128), F32),
            vmem((8, 128), F32),
            vmem((NY, 8, 128), F32),
            vmem((8, 128), F32),
            vmem((NZ, 8, 128), F32),
            vmem((NDP, 8, BW), F32),
            vmem((NDP, 8, BW), F32),
            vmem((8, 128), F32),
            vmem((NDP, 8, 128), F32),
            vmem((8, S), F32),
            dma((NG,)),
            dma((9,)),
            dma((NY * NZ,)),
            dma((NY * NZ,)),
            dma((NY * NZ,)),
            dma((NY * NZ,)),
            dma((3,)),
            dma((20,)),
        ],
        compiler_params=pltpu.CompilerParams(
            collective_id=0, has_side_effects=True, vmem_limit_bytes=63 * 1024 * 1024
        ),
        name="critic",
    )(
        hidden,
        norm_gain,
        w_in,
        w_out,
        rewards,
        old_values,
        send_slot,
        pack_slot,
        positions,
        episode_len,
    )


def solution(mesh):
    both = P("dp", "context")
    return jax.shard_map(
        local,
        mesh=mesh,
        in_specs=(P("dp", "context", None), P("context"), P("context", None), P()) + (both,) * 6,
        out_specs=(both, both),
        check_vma=False,
    )
```

```python
import jax
import jax.numpy as jnp
from jax import lax
from jax.experimental import pallas as pl
from jax.experimental.pallas import tpu as pltpu
from jax.sharding import PartitionSpec as P

F32 = jnp.float32
BF16 = jnp.bfloat16
MESH = pl.DeviceIdType.MESH

NX, NY, NZ = 4, 4, 8
NDP = 2 * NX
T = 768
S = 1536
D = 8192
VH = 512
KB = 256
BUCKET = 192
BW = 256
GB = 4
NG = 8
KG = GB * KB
EPS = 1e-05

HALF = KB // 2
XR = 48
TREE = HALF - XR

BLOCKS = [
    (0, 0), (-1, 0), (0, 1), (0, -1), (1, 0), (0, 2), (0, -2), (1, 1),
    (-1, 1), (1, -2), (-1, -2), (1, -1), (0, -3), (-1, -1), (1, 2), (-1, 2),
    (2, 0), (0, 3), (2, -2), (2, 2), (2, 1), (-1, -3), (1, -3), (2, -1),
    (0, 4), (1, 4), (1, 3), (-1, 4), (-1, 3), (2, -3), (2, 4), (2, 3),
]
GROUPS = [BLOCKS[GB * g : GB * g + GB] for g in range(NG)]
SLOT = {b: i for i, b in enumerate(BLOCKS)}
PARTS = [(GB * g, GB * g + GB) for g in range(NG - 1)] + [(28, 30), (30, 32)]

PLAN = [
    ('load', 0),
    ('load', 1),
    ('load', 2),
    ('load', 3),
    ('load', 4),
    ('load', 5),
    ('load', 6),
    ('load', 7),
    ('to_rows',),
    ('coefficients',),
    ('pack_table',),
    ('tails',),
    ((4,), ()),
    ((1, 2, 3), ()),
    ((65, 66, 67), ()),
    ('squares', 0, 0),
    ('squares', 0, 1),
    ((), (1,)),
    ((), (65,)),
    ((68,), ()),
    ((16,), ()),
    ('squares', 1, 0),
    ('squares', 1, 1),
    ((), (5,)),
    ((), (6, 2, 3)),
    ((80,), ()),
    ('squares', 2, 0),
    ((), (4,)),
    ('squares', 2, 1),
    ((), (68,)),
    ((), (66, 67)),
    ((), (69, 70)),
    ((7,), ()),
    ((11,), ()),
    ('squares', 3, 0),
    ('squares', 3, 1),
    ((36, 8, 13), ()),
    ('at_rows',),
    ((33, 5, 6), ()),
    ((72, 77), ()),
    ('returns_scan',),
    ((34, 69, 70), ()),
    ((35, 71, 75), ()),
    ('squares', 4, 0),
    ('squares', 4, 1),
    ((48, 20, 23), ()),
    ('squares', 5, 0),
    ((), (33,)),
    ('squares', 5, 1),
    ('squares', 6, 0),
    ((87,), (14, 15)),
    ('squares', 6, 1),
    ((), (9,)),
    ((), (37, 10)),
    ((), (7,)),
    ((), (38, 8, 12)),
    ((), (11,)),
    ((), (34, 13)),
    ((), (76,)),
    ((), (72,)),
    ('squares', 7, 0),
    ((), (35, 16, 24, 17, 77)),
    ((), (80, 79)),
    ((), (36,)),
    ((), (71,)),
    ('squares', 7, 1),
    ((39,), (74, 75)),
    ('inverse',),
    ((9, 84), (78, 81)),
    ((43,), (88,)),
    ((), (73,)),
    ((10,), ()),
    ((40,), ()),
    ((12,), ()),
    ((74,), ()),
    ((45,), ()),
    ((14,), ()),
    ((76,), ()),
    ((), (46,)),
    ((), (19,)),
    ((), (18,)),
    ((37,), ()),
    ((73,), ()),
    ((15,), ()),
    ('matmul', 0, 0, 0),
    ((38, 18, 17), (47, 20)),
    ((82,), (21,)),
    ((52, 79), ()),
    ('matmul', 0, 0, 1),
    ((81,), (41, 22)),
    ((55,), (23,)),
    ('carry_z',),
    ((78,), (86,)),
    ((22,), (42, 85)),
    ('matmul', 0, 1, 0),
    ((19,), (25,)),
    ((21,), (39, 27)),
    ((41,), ()),
    ((83,), ()),
    ('matmul', 0, 1, 1),
    ((42, 85), (26,)),
    ((), (40, 28)),
    ('tails_in',),
    ((44, 26), (44, 84, 87)),
    ((86,), (83,)),
    ((), (82,)),
    ((), (90,)),
    ((), (43, 92)),
    ((), (89,)),
    ((), (91,)),
    ((28,), ()),
    ((46,), ()),
    ((), (45,)),
    ((), (29,)),
    ('matmul', 1, 0, 0),
    ((47, 29, 24), (48,)),
    ((), (93,)),
    ((), (56,)),
    ('matmul', 1, 0, 1),
    ((93, 92), ()),
    ((50,), ()),
    ('matmul', 1, 1, 0),
    ((88,), (49, 30)),
    ('matmul', 1, 1, 1),
    ((49, 90, 25), (31,)),
    ((), (51,)),
    ('matmul', 2, 0, 0),
    ((54, 31, 27), (50,)),
    ('matmul', 2, 0, 1),
    ((95, 91), (95,)),
    ('matmul', 2, 1, 0),
    ((51,), (52,)),
    ('matmul', 2, 1, 1),
    ((53, 89), (94,)),
    ('matmul', 3, 0, 0),
    ((58,), (53,)),
    ('matmul', 3, 0, 1),
    ((), (54,)),
    ('matmul', 3, 1, 0),
    ((60, 30), ()),
    ('matmul', 3, 1, 1),
    ((94,), (55,)),
    ((61,), ()),
    ((), (57,)),
    ((56,), ()),
    ((), (59,)),
    ('returns_done',),
    ('matmul', 4, 0, 0),
    ('matmul', 4, 0, 1),
    ((), (58,)),
    ('matmul', 4, 1, 0),
    ((57,), ()),
    ('matmul', 4, 1, 1),
    ((), (60,)),
    ((63,), ()),
    ((59,), ()),
    ((), (61,)),
    ((), (62,)),
    ('matmul', 5, 0, 0),
    ('matmul', 5, 0, 1),
    ('matmul', 5, 1, 0),
    ((), (63,)),
    ('matmul', 5, 1, 1),
    ((62,), ()),
    ('matmul', 6, 0, 0),
    ('matmul', 6, 0, 1),
    ('matmul', 6, 1, 0),
    ('matmul', 6, 1, 1),
    ('matmul', 7, 0, 0),
    ('matmul', 7, 0, 1),
    ('matmul', 7, 1, 0),
    ('matmul', 7, 1, 1),
    ('matmul', 8, 0, 0),
    ('matmul', 8, 0, 1),
    ('matmul', 8, 1, 0),
    ('matmul', 8, 1, 1),
]


def children_yz(dy, dz):
    out = []
    if dz == 0 and dy == 0:
        out += [((1, 0), 1), ((-1, 0), 1), ((1, 0), 2)]
    if dz in (0, 1, 2) or (dz == 3 and dy == 0):
        out += [((0, 1), 1)]
    if dz in (0, -1, -2) or (dz == -3 and dy != 0):
        out += [((0, -1), 1)]
    return out


def children_zy(dy, dz):
    out = []
    if dy == 0:
        if dz == 0:
            out += [((0, 1), 2), ((0, -1), 2), ((0, 1), 1), ((0, -1), 1)]
        elif dz == 2:
            out += [((0, 1), 2), ((0, 1), 1)]
        elif dz == -2:
            out += [((0, -1), 1)]
        out += [((1, 0), 1), ((-1, 0), 1)]
    elif dy == 1 and dz in (0, 1, 2, 3):
        out += [((1, 0), 1)]
    elif dy == -1 and dz in (-1, -2, -3, 4):
        out += [((-1, 0), 1)]
    return out


def after(b, step, hops):
    dy, dz = b[0] + step[0] * hops, b[1] + step[1] * hops
    return (2 if dy == -2 else dy, 4 if dz == -4 else dz)


def split3(v):
    hi = v.astype(BF16).astype(F32)
    rest = v - hi
    mid = rest.astype(BF16).astype(F32)
    return hi, mid, rest - mid


def rows_of(parts, width):
    row = lax.broadcasted_iota(jnp.int32, (8, width), 0)
    out = jnp.zeros((8, width), F32)
    for i, part in enumerate(parts):
        out = jnp.where(row == i, jnp.broadcast_to(part, (8, width)), out)
    return out


def quotient(s):
    q = jnp.zeros_like(s)
    for i in range(1, NDP):
        q = q + (s >= BUCKET * i).astype(jnp.int32)
    return q


def spread(parts, q):
    return jnp.concatenate(
        [jnp.where(q == r, parts, 0.0) for r in range(NDP)], axis=0
    ).astype(BF16)


def collect(table, q):
    out = jnp.where(q == 0, table[0:8], 0.0)
    for r in range(1, NDP):
        out = out + jnp.where(q == r, table[8 * r : 8 * r + 8], 0.0)
    return out


def nt_dot(a, b):
    return lax.dot_general(a, b, (((1,), (1,)), ((), ())), preferred_element_type=F32)


def kernel(
    hid_hbm, gain_hbm, win_hbm, wout_hbm, rew_hbm, old_hbm, send_hbm, pack_hbm, pos_hbm, len_hbm,
    adv_out, loss_out,
    hid, wall, acc, ssq, inv, gain_in, win, wout, rew, old, send, pack, pos, elen,
    hot_send, hot_pack, osend, oland, rsend, rland, lev, tail_a, rowdat,
    first_a, esend, eland, weight, csend, cland, tsend, tland, isend, iland, own,
    sem_hid, sem_small, tree_recv, rest_recv, x_recv, sib_recv, sem_sent, sem_ex,
):
    dp = lax.axis_index("dp")
    ctx = lax.axis_index("context")
    y = lax.rem(ctx, NY)
    z = lax.div(ctx, NY)
    core = lax.rem(dp, 2)
    even = 1 - lax.rem(lax.div(dp, 2), 2)

    def ctx_at(dy, dz):
        return lax.rem(z + dz + NZ, NZ) * NY + lax.rem(y + dy + NY, NY)

    def dp_at(step):
        return lax.rem(dp + step + NDP, NDP)

    sibling = dp + 1 - 2 * core

    def at(dy, dz):
        return (dp, ctx_at(dy, dz))

    smalls = [
        (send_hbm, send), (rew_hbm, rew), (old_hbm, old), (pack_hbm, pack),
        (gain_hbm, gain_in), (pos_hbm, pos), (len_hbm, elen), (wout_hbm, wout), (win_hbm, win),
    ]
    small_copies = [
        pltpu.make_async_copy(src, dst, sem_small.at[i]) for i, (src, dst) in enumerate(smalls)
    ]
    small_copies[8].start()
    small_copies[4].start()

    barrier = pltpu.get_barrier_semaphore()

    peers = [at(k, 0) for k in range(1, NY)] + [at(0, k) for k in range(1, NZ)]
    peers += [(dp_at(k), ctx) for k in range(1, NDP)]
    for peer in peers:
        pl.semaphore_signal(barrier, inc=1, device_id=peer, device_id_type=MESH)
    for i in (0, 1, 2, 3, 5, 6, 7):
        small_copies[i].start()

    small_copies[4].wait()
    small_copies[8].wait()
    square = (KB, KB)
    diagonal = lax.broadcasted_iota(jnp.int32, square, 0) == lax.broadcasted_iota(
        jnp.int32, square, 1
    )
    gains = jnp.broadcast_to(gain_in[...].astype(F32).reshape(1, KB), square)
    wall[0] = jnp.dot(
        jnp.where(diagonal, gains, 0.0).astype(BF16), win[...], preferred_element_type=F32
    ).astype(BF16)

    def load(g):
        for j in range(GB):
            b = GROUPS[g][j]
            column = pl.multiple_of(ctx_at(-b[0], -b[1]) * KB, KB)
            pltpu.make_async_copy(
                hid_hbm.at[0, :, pl.ds(column, KB)], hid.at[g, :, pl.ds(j * KB, KB)], sem_hid.at[g]
            ).start()

    pl.semaphore_wait(barrier, len(peers))

    base = HALF * core
    rest_rows = pl.ds(pl.multiple_of(base + XR, 16), TREE - XR)
    x_rows = pl.ds(pl.multiple_of(base + TREE * even, 16), XR)
    x_lands = pl.ds(pl.multiple_of(base + TREE * (1 - even), 16), XR)
    half_rows = pl.ds(pl.multiple_of(base, 16), HALF)
    other_rows = pl.ds(pl.multiple_of(HALF - base, 16), HALF)
    x_peer = (dp_at(2 - 4 * core), ctx)

    def tree_step(c, b, first):
        slot = SLOT[b]
        rows = x_rows if first else rest_rows
        arrived = tree_recv if first else rest_recv
        if slot:
            here = wall.at[slot, rows]
            pltpu.make_async_copy(here, here, arrived.at[slot]).wait()
        for step, hops in (children_yz if c == 0 else children_zy)(*b):
            to = SLOT[after(b, step, hops)]
            pltpu.make_async_remote_copy(
                src_ref=wall.at[slot, rows],
                dst_ref=wall.at[to, rows],
                send_sem=sem_sent.at[0],
                recv_sem=arrived.at[to],
                device_id=at(step[0] * hops, step[1] * hops),
                device_id_type=MESH,
            ).start()
        if slot and first:
            part = wall.at[slot, x_rows]
            pltpu.make_async_remote_copy(
                src_ref=part,
                dst_ref=part,
                send_sem=sem_sent.at[1],
                recv_sem=x_recv.at[slot],
                device_id=x_peer,
                device_id_type=MESH,
            ).start()

    def x_step(slot):
        part = wall.at[slot, x_lands]
        pltpu.make_async_copy(part, part, x_recv.at[slot]).wait()

    def hand_over(slot):
        part = wall.at[slot, half_rows]
        pltpu.make_async_remote_copy(
            src_ref=part,
            dst_ref=part,
            send_sem=sem_sent.at[2],
            recv_sem=sib_recv.at[slot],
            device_id=(sibling, ctx),
            device_id_type=MESH,
        ).start()

    def handed(slot):
        part = wall.at[slot, other_rows]
        pltpu.make_async_copy(part, part, sib_recv.at[slot]).wait()

    seen = [set(), set()]

    def arrivals(c, codes):
        for code in codes:
            slot = code % 32
            if code // 32 == 1:
                x_step(slot)
            else:
                tree_step(c, BLOCKS[slot], code < 32)
            seen[c].add(code)
            if {slot, slot + 32, slot + 64} <= seen[c]:
                hand_over(slot)

    def by_core(first, second):
        if first:

            @pl.when(core == 0)
            def _():
                arrivals(0, first)

        if second:

            @pl.when(core == 1)
            def _():
                arrivals(1, second)

    def exchange(pairs, send_sem, recv_sem):
        for src, dst, device in pairs:
            pltpu.make_async_remote_copy(
                src_ref=src, dst_ref=dst, send_sem=send_sem, recv_sem=recv_sem,
                device_id=device, device_id_type=MESH,
            ).start()

    def await_bytes(ref, sem):
        pltpu.make_async_copy(ref, ref, sem).wait()

    def along_context(src, land, sem):
        def one(k, _):
            pltpu.make_async_remote_copy(
                src_ref=src, dst_ref=land.at[pl.ds(ctx, 1)],
                send_sem=sem_ex.at[sem], recv_sem=sem_ex.at[sem + 1],
                device_id=(dp, lax.rem(ctx + NY * NZ - k, NY * NZ)), device_id_type=MESH,
            ).start()
            return 0

        lax.fori_loop(1, NY * NZ, one, 0)

    def along_dp(src, dst, sem):
        exchange(
            [(src.at[dp_at(k)], dst, (dp_at(k), ctx)) for k in range(1, NDP)],
            sem_ex.at[sem],
            sem_ex.at[sem + 1],
        )

    def to_rows():
        for i in range(3):
            small_copies[i].wait()
        s = send[...]
        q = quotient(s)
        k = s - BUCKET * q
        hot_send[...] = (
            lax.broadcasted_iota(jnp.int32, (BW, S), 0) == jnp.broadcast_to(k, (BW, S))
        ).astype(F32).astype(BF16)
        parts = rows_of(split3(rew[...]) + split3(old[...]), S)
        table = nt_dot(spread(parts, q), hot_send[...])
        for r in range(NDP):
            osend[r] = table[8 * r : 8 * r + 8]
        along_dp(osend, oland.at[dp], 4)
        oland[pl.ds(dp, 1)] = osend[pl.ds(dp, 1)]

    def pack_table():
        small_copies[3].wait()
        s = pack[...]
        k = s - BUCKET * quotient(s)
        hot_pack[...] = (
            lax.broadcasted_iota(jnp.int32, (BW, T), 0) == jnp.broadcast_to(k, (BW, T))
        ).astype(F32).astype(BF16)

    def at_rows():
        await_bytes(oland.at[pl.ds(0, NDP - 1)], sem_ex.at[5])
        table = oland[...].reshape(8 * NDP, BW).astype(BF16)
        got = collect(
            jnp.dot(table, hot_pack[...], preferred_element_type=F32), quotient(pack[...])
        )
        rowdat[0] = jnp.broadcast_to(got[0:1] + got[1:2] + got[2:3], (8, T))
        rowdat[1] = jnp.broadcast_to(got[3:4] + got[4:5] + got[5:6], (8, T))

    lane = lax.broadcasted_iota(jnp.int32, (8, T), 1)
    row8 = lax.broadcasted_iota(jnp.int32, (8, T), 0)
    strides = [(1, 3), (4, 3), (16, 3), (64, 3), (256, 2)]

    def later(v, d, fill):
        return jnp.where(lane < T - d, pltpu.roll(v, T - d, 1), fill)

    def wide(slab):
        return jnp.concatenate([slab] * (T // 128), axis=1)

    def slab_of(v):
        return jnp.broadcast_to(v[:, 0:1], (8, 128))

    def coefficients():
        small_copies[5].wait()
        small_copies[6].wait()
        keep = jnp.where(pos[...] == 0, 0.0, 1.0).astype(F32)
        below = elen[...].astype(F32) + 20.0
        lost = 20.0 / below
        lost = lost + lost * (20.0 - lost * below) * 0.05
        keep8 = jnp.broadcast_to(keep, (8, T))
        lost8 = jnp.broadcast_to(lost, (8, T))
        rowdat[2] = keep8
        rowdat[3] = lost8
        a = jnp.where(row8 == 1, keep8, keep8 * (1.0 - lost8))
        i = 0
        for d, count in strides:
            reach = a
            for k in range(1, count + 1):
                lev[i] = jnp.where(lane < T - k * d, reach, 0.0)
                reach = reach * later(a, k * d, 1.0)
                i += 1
            a = reach
        tail_a[...] = later(a, 1, 1.0)
        first_a[...] = slab_of(a)

    def scan(b):
        i = 0
        for d, count in strides:
            total = b
            for k in range(1, count + 1):
                total = total + lev[i] * pltpu.roll(b, T - k * d, 1)
                i += 1
            b = total
        return b

    def tails():
        table = nt_dot(
            spread(rows_of(split3(tail_a[0:1]), T), quotient(pack[...])), hot_pack[...]
        )
        for r in range(NDP):
            tsend[r] = table[8 * r : 8 * r + 8]
        along_dp(tsend, tland.at[dp], 16)
        tland[pl.ds(dp, 1)] = tsend[pl.ds(dp, 1)]

    def to_owner(land):
        table = land[...].reshape(8 * NDP, BW).astype(BF16)
        return collect(
            jnp.dot(table, hot_send[...], preferred_element_type=F32), quotient(send[...])
        )

    def tails_in():
        await_bytes(tland.at[pl.ds(0, NDP - 1)], sem_ex.at[17])
        got = to_owner(tland)
        own[0:1] = got[0:1] + got[1:2] + got[2:3]

    def returns_scan():
        b = scan(jnp.where(row8 == 1, rowdat[2] * rowdat[0], 0.0))
        rowdat[4] = later(b, 1, 0.0)
        esend[0] = jnp.concatenate([first_a[0:1], first_a[1:2], slab_of(b)[1:2]], axis=1)
        eland[pl.ds(ctx, 1)] = esend[...]
        exchange(
            [(esend, eland.at[pl.ds(ctx, 1)], at(k, 0)) for k in range(1, NY)], sem_ex.at[6], sem_ex.at[7]
        )

    def carry_z():
        await_bytes(eland.at[pl.ds(0, NY - 1)], sem_ex.at[7])
        mine = eland.at[pl.ds(pl.multiple_of(z * NY, NY), NY)]
        exchange([(mine, mine, at(0, k)) for k in range(1, NZ)], sem_ex.at[8], sem_ex.at[9])

    def returns_done():
        await_bytes(eland.at[pl.ds(0, NY * (NZ - 1))], sem_ex.at[9])
        inflow = jnp.zeros((1, 128), F32)
        for i in reversed(range(NY * NZ)):
            inflow = jnp.where(
                i > ctx, eland[i, :, 256:384] + eland[i, :, 128:256] * inflow, inflow
            )
        reach = jnp.ones((1, 128), F32)
        for i in range(NY * NZ):
            weight[i] = jnp.where(i > ctx, reach, 0.0)
            reach = jnp.where(i > ctx, reach * eland[i, :, 0:128], reach)
        ret = rowdat[0] + tail_a[1:2] * wide(inflow) + rowdat[4]
        rowdat[5] = jnp.broadcast_to(ret[1:2], (8, T))
        keep8, lost8 = rowdat[2], rowdat[3]
        rowdat[6] = keep8 * (1.0 - lost8) * rowdat[0]
        rowdat[7] = keep8 * lost8

    TR = 32

    def over_rows(body, half):
        def one(i, _):
            body(pl.ds(pl.multiple_of(half * (T // 2) + i * TR, TR), TR))
            return 0

        lax.fori_loop(0, T // 2 // TR, one, 0)

    def squares(g, half):
        if half == 0:
            pltpu.make_async_copy(hid.at[g], hid.at[g], sem_hid.at[g]).wait()

        def body(rows):
            v = hid[g, rows, :].astype(F32)
            v = v * v
            total = v[:, 0:128]
            for j in range(1, KG // 128):
                total = total + v[:, 128 * j : 128 * j + 128]
            ssq[rows, :] = total if g == 0 else ssq[rows, :] + total

        over_rows(body, half)

    def inverse():
        def body(i, _):
            rows = pl.ds(pl.multiple_of(i * 128, 128), 128)
            mean = jnp.sum(ssq[rows, :], axis=1, keepdims=True) * (1.0 / D)
            inv[rows, :] = jnp.broadcast_to(lax.rsqrt(mean + EPS), (128, 128))
            return 0

        lax.fori_loop(0, T // 128, body, 0)

    def matmul(part, half, upper):
        first, end = PARTS[part]
        rows = slice(T // 2 * upper, T // 2 * upper + T // 2)
        if half == 0 and upper == 0:
            for slot in range(first, end):
                if slot:
                    handed(slot)
        cols = slice(256 * half, 256 * half + 256)
        w = wall[first:end, :, cols].reshape(KB * (end - first), 256)
        g, offset = divmod(first * KB, KG)
        v = jnp.dot(
            hid[g, rows, offset : offset + KB * (end - first)], w, preferred_element_type=F32
        )
        acc[rows, cols] = v if part == 0 else acc[rows, cols] + v

    items = dict(
        load=load, to_rows=to_rows, coefficients=coefficients, tails=tails,
        pack_table=pack_table, at_rows=at_rows, returns_scan=returns_scan, carry_z=carry_z,
        returns_done=returns_done, squares=squares, inverse=inverse,
        matmul=matmul, tails_in=tails_in,
    )
    for c in range(2):

        @pl.when(core == c)
        def _(c=c):
            tree_step(c, (0, 0), True)
            tree_step(c, (0, 0), False)

    for step in PLAN:
        if isinstance(step[0], str):
            items[step[0]](*step[1:])
        else:
            by_core(*step)

    for i in (7,):
        small_copies[i].wait()
    w_row = jnp.broadcast_to(wout[...].astype(F32).reshape(1, VH), (16, VH)).astype(BF16)

    def activate(i, _):
        rows = pl.ds(pl.multiple_of(i * 128, 128), 128)
        half = acc[rows, :] * jnp.concatenate([inv[rows, :] * 0.5] * (VH // 128), axis=1)
        act = (half * jnp.tanh(half) + half).astype(BF16)
        hid[0, rows, 0:VH] = act
        return 0

    lax.fori_loop(0, T // 128, activate, 0)
    values = nt_dot(w_row, hid[0, :, 0:VH])[0:8]

    b = scan(rowdat[7] * values + rowdat[6])
    csend[0] = slab_of(b)[0:1]
    along_context(csend, cland, 10)
    cland[pl.ds(ctx, 1)] = csend[...]
    base_adv = rowdat[0] - values + later(b, 1, 0.0)
    old_row, ret = rowdat[1], rowdat[5]
    clipped = old_row + jnp.clip(values - old_row, -0.2, 0.2)
    loss = 0.5 * jnp.maximum(jnp.square(values - ret), jnp.square(clipped - ret))
    parts = rows_of(split3(base_adv[0:1]) + split3(loss[0:1]), T)
    table = nt_dot(spread(parts, quotient(pack[...])), hot_pack[...])
    for r in range(NDP):
        rsend[r] = table[8 * r : 8 * r + 8]
    along_dp(rsend, rland.at[dp], 14)
    rland[pl.ds(dp, 1)] = rsend[pl.ds(dp, 1)]

    q = quotient(send[...])
    await_bytes(rland.at[pl.ds(0, NDP - 1)], sem_ex.at[15])
    got = to_owner(rland)
    own[1:2] = got[0:1] + got[1:2] + got[2:3]
    old[...] = got[3:4] + got[4:5] + got[5:6]
    loss_copy = pltpu.make_async_copy(old, loss_out, sem_small.at[1])
    loss_copy.start()
    await_bytes(cland.at[pl.ds(0, NY * NZ - 1)], sem_ex.at[11])
    inflow = weight[0] * cland[0]
    for i in range(1, NY * NZ):
        inflow = inflow + weight[i] * cland[i]
    inflow = jnp.broadcast_to(inflow, (8, 128))
    isend[...] = inflow
    iland[pl.ds(dp, 1)] = inflow[None]
    exchange(
        [(isend, iland.at[dp], (dp_at(k), ctx)) for k in range(1, NDP)], sem_ex.at[18], sem_ex.at[19]
    )

    await_bytes(wall.at[pl.ds(0, 31), pl.ds(0, TREE)], sem_sent.at[0])
    await_bytes(wall.at[pl.ds(0, 31), pl.ds(0, XR)], sem_sent.at[1])
    await_bytes(wall.at[pl.ds(0, 31), pl.ds(0, HALF)], sem_sent.at[2])
    await_bytes(oland.at[pl.ds(0, NDP - 1)], sem_ex.at[4])
    await_bytes(eland.at[pl.ds(0, NY - 1)], sem_ex.at[6])
    await_bytes(eland.at[pl.ds(0, NY * (NZ - 1))], sem_ex.at[8])
    await_bytes(cland.at[pl.ds(0, NY * NZ - 1)], sem_ex.at[10])
    await_bytes(rland.at[pl.ds(0, NDP - 1)], sem_ex.at[14])
    await_bytes(tland.at[pl.ds(0, NDP - 1)], sem_ex.at[16])

    await_bytes(iland.at[pl.ds(0, NDP - 1)], sem_ex.at[19])
    flow = jnp.zeros((1, S), F32)
    for r in range(NDP):
        here = jnp.concatenate([iland[r, 0:1]] * (S // 128), axis=1)
        flow = flow + jnp.where(q == r, here, 0.0)
    rew[...] = own[1:2] + own[0:1] * flow
    adv_copy = pltpu.make_async_copy(rew, adv_out, sem_small.at[0])
    adv_copy.start()
    await_bytes(iland.at[pl.ds(0, NDP - 1)], sem_ex.at[18])
    loss_copy.wait()
    adv_copy.wait()


def local(
    hidden, norm_gain, w_in, w_out, rewards, old_values, send_slot, pack_slot, positions, episode_len
):
    outside = pl.BlockSpec(memory_space=pltpu.HBM)
    vmem = pltpu.VMEM
    dma = pltpu.SemaphoreType.DMA
    return pl.pallas_call(
        kernel,
        out_shape=(jax.ShapeDtypeStruct((1, S), F32), jax.ShapeDtypeStruct((1, S), F32)),
        in_specs=[outside] * 10,
        out_specs=(outside, outside),
        scratch_shapes=[
            vmem((NG, T, KG), BF16),
            vmem((NY * NZ, KB, VH), BF16),
            vmem((T, VH), F32),
            vmem((T, 128), F32),
            vmem((T, 128), F32),
            vmem((KB,), BF16),
            vmem((KB, VH), BF16),
            vmem((VH,), BF16),
            vmem((1, S), F32),
            vmem((1, S), F32),
            vmem((1, S), jnp.int32),
            vmem((1, T), jnp.int32),
            vmem((1, T), jnp.int32),
            vmem((1, T), jnp.int32),
            vmem((BW, S), BF16),
            vmem((BW, T), BF16),
            vmem((NDP, 8, BW), F32),
            vmem((NDP, 8, BW), F32),
            vmem((NDP, 8, BW), F32),
            vmem((NDP, 8, BW), F32),
            vmem((14, 8, T), F32),
            vmem((8, T), F32),
            vmem((8, 8, T), F32),
            vmem((8, 128), F32),
            vmem((1, 1, 384), F32),
            vmem((NY * NZ, 1, 384), F32),
            vmem((NY * NZ, 1, 128), F32),
            vmem((1, 1, 128), F32),
            vmem((NY * NZ, 1, 128), F32),
            vmem((NDP, 8, BW), F32),
            vmem((NDP, 8, BW), F32),
            vmem((8, 128), F32),
            vmem((NDP, 8, 128), F32),
            vmem((8, S), F32),
            dma((NG,)),
            dma((9,)),
            dma((NY * NZ,)),
            dma((NY * NZ,)),
            dma((NY * NZ,)),
            dma((NY * NZ,)),
            dma((3,)),
            dma((20,)),
        ],
        compiler_params=pltpu.CompilerParams(
            collective_id=0, has_side_effects=True, vmem_limit_bytes=63 * 1024 * 1024
        ),
        name="critic",
    )(
        hidden,
        norm_gain,
        w_in,
        w_out,
        rewards,
        old_values,
        send_slot,
        pack_slot,
        positions,
        episode_len,
    )


def solution(mesh):
    both = P("dp", "context")
    return jax.shard_map(
        local,
        mesh=mesh,
        in_specs=(P("dp", "context", None), P("context"), P("context", None), P()) + (both,) * 6,
        out_specs=(both, both),
        check_vma=False,
    )
```

```python
import jax
import jax.numpy as jnp
from jax import lax
from jax.experimental import pallas as pl
from jax.experimental.pallas import tpu as pltpu
from jax.sharding import PartitionSpec as P

F32 = jnp.float32
BF16 = jnp.bfloat16
MESH = pl.DeviceIdType.MESH

NX, NY, NZ = 4, 4, 8
NDP = 2 * NX
T = 768
S = 1536
D = 8192
VH = 512
KB = 256
BUCKET = 192
BW = 256
GB = 4
NG = 8
KG = GB * KB
EPS = 1e-05

HALF = KB // 2
XR = 48
TREE = HALF - XR

BLOCKS = [
    (0, 0), (-1, 0), (0, 1), (0, -1), (1, 0), (0, 2), (0, -2), (1, 1),
    (-1, 1), (1, -2), (1, -1), (-1, -2), (-1, -1), (0, -3), (2, 0), (1, 2),
    (-1, 2), (2, -2), (0, 3), (2, 1), (2, 2), (-1, -3), (1, -3), (2, -1),
    (0, 4), (1, 4), (1, 3), (-1, 3), (2, -3), (-1, 4), (2, 3), (2, 4),
]
GROUPS = [BLOCKS[GB * g : GB * g + GB] for g in range(NG)]
SLOT = {b: i for i, b in enumerate(BLOCKS)}
PARTS = [(GB * g, GB * g + GB) for g in range(NG - 1)] + [(28, 30), (30, 32)]

PLAN = [
    ('load', 0),
    ('load', 1),
    ('load', 2),
    ('load', 3),
    ('load', 4),
    ('load', 5),
    ('load', 6),
    ('load', 7),
    ('to_rows',),
    ('coefficients',),
    ('pack_table',),
    ('tails',),
    ((4,), ()),
    ((1, 2, 3), ()),
    ((65, 66, 67), ()),
    ('squares', 0, 0),
    ('squares', 0, 1),
    ((), (1,)),
    ((), (65,)),
    ((68,), ()),
    ((14,), ()),
    ('squares', 1, 0),
    ('squares', 1, 1),
    ((), (5,)),
    ((), (6, 2, 3)),
    ((78,), ()),
    ('squares', 2, 0),
    ((), (4,)),
    ('squares', 2, 1),
    ((), (68,)),
    ((), (66, 67)),
    ((), (69, 70)),
    ((7,), ()),
    ((10,), ()),
    ('squares', 3, 0),
    ((36,), ()),
    ('squares', 3, 1),
    ((8, 12), ()),
    ('at_rows',),
    ((33, 5, 6), ()),
    ((34, 72, 76), ()),
    ('returns_scan',),
    ((35, 69, 70), ()),
    ((71, 74), ()),
    ('squares', 4, 0),
    ((46,), ()),
    ('squares', 4, 1),
    ((19, 23), (33,)),
    ('squares', 5, 0),
    ('squares', 5, 1),
    ('squares', 6, 0),
    ((87,), (15, 16)),
    ('squares', 6, 1),
    ((), (37,)),
    ((), (9,)),
    ((), (11,)),
    ((), (38,)),
    ((), (7,)),
    ((), (8, 13)),
    ((), (34,)),
    ((), (10,)),
    ((), (12,)),
    ((), (77,)),
    ((), (35, 72)),
    ((), (14,)),
    ((), (24, 18)),
    ((), (36, 76, 78)),
    ('squares', 7, 0),
    ((39,), (80, 71)),
    ('squares', 7, 1),
    ((), (75, 74)),
    ('inverse',),
    ((42, 9, 83), (79, 82)),
    ((), (88,)),
    ((), (73,)),
    ('matmul', 0, 0, 0),
    ((40, 11, 44, 13, 75), (47, 17)),
    ((15, 77), (20,)),
    ((37,), ()),
    ('matmul', 0, 0, 1),
    ((73,), (48,)),
    ((16,), ()),
    ((38,), ()),
    ('matmul', 0, 1, 0),
    ((17,), (19, 21)),
    ((18,), (41,)),
    ((51,), ()),
    ((81,), ()),
    ((80,), ()),
    ('matmul', 0, 1, 1),
    ((55, 82), (22, 23)),
    ('carry_z',),
    ((), (43, 86)),
    ((), (85,)),
    ('tails_in',),
    ((79, 22), (39, 25, 29)),
    ((), (40,)),
    ((20,), ()),
    ((41,), ()),
    ((), (26,)),
    ((), (27,)),
    ((84,), ()),
    ((), (83,)),
    ((), (45, 87)),
    ((), (84,)),
    ((), (81,)),
    ((21,), ()),
    ((), (42,)),
    ((), (90,)),
    ((), (91,)),
    ('matmul', 1, 0, 0),
    ((43, 26, 85), (44, 89, 93)),
    ((86,), ()),
    ((27,), ()),
    ((45,), ()),
    ('matmul', 1, 0, 1),
    ((28,), (46, 28)),
    ((47, 24), ()),
    ('matmul', 1, 1, 0),
    ((92, 91), ()),
    ('matmul', 1, 1, 1),
    ((48, 88), (56, 92)),
    ('matmul', 2, 0, 0),
    ((49, 90), (50,)),
    ('matmul', 2, 0, 1),
    ((25,), (31,)),
    ((50, 30), (49,)),
    ('matmul', 2, 1, 0),
    ((94,), (30,)),
    ((54,), ()),
    ('matmul', 2, 1, 1),
    ((29,), (52,)),
    ('matmul', 3, 0, 0),
    ((52, 93), (51, 94)),
    ('matmul', 3, 0, 1),
    ((53, 89), ()),
    ('matmul', 3, 1, 0),
    ((), (53, 95)),
    ('matmul', 3, 1, 1),
    ((58, 31), ()),
    ((), (54,)),
    ((), (55,)),
    ((95,), ()),
    ('matmul', 4, 0, 0),
    ((59,), ()),
    ('matmul', 4, 0, 1),
    ((60,), ()),
    ('returns_done',),
    ((), (57,)),
    ('matmul', 4, 1, 0),
    ((56,), (61,)),
    ('matmul', 4, 1, 1),
    ((57,), ()),
    ('matmul', 5, 0, 0),
    ((), (58,)),
    ('matmul', 5, 0, 1),
    ((62,), (59,)),
    ('matmul', 5, 1, 0),
    ((61,), ()),
    ('matmul', 5, 1, 1),
    ((), (60,)),
    ((), (63,)),
    ((), (62,)),
    ((63,), ()),
    ('matmul', 6, 0, 0),
    ('matmul', 6, 0, 1),
    ('matmul', 6, 1, 0),
    ('matmul', 6, 1, 1),
    ('matmul', 7, 0, 0),
    ('matmul', 7, 0, 1),
    ('matmul', 7, 1, 0),
    ('matmul', 7, 1, 1),
    ('matmul', 8, 0, 0),
    ('matmul', 8, 0, 1),
    ('matmul', 8, 1, 0),
    ('matmul', 8, 1, 1),
]


def children_yz(dy, dz):
    out = []
    if dz == 0 and dy == 0:
        out += [((1, 0), 1), ((-1, 0), 1), ((1, 0), 2)]
    if dz in (0, 1, 2) or (dz == 3 and dy == 0):
        out += [((0, 1), 1)]
    if dz in (0, -1, -2) or (dz == -3 and dy != 0):
        out += [((0, -1), 1)]
    return out


def children_zy(dy, dz):
    out = []
    if dy == 0:
        if dz == 0:
            out += [((0, 1), 2), ((0, -1), 2), ((0, 1), 1), ((0, -1), 1)]
        elif dz == 2:
            out += [((0, 1), 2), ((0, 1), 1)]
        elif dz == -2:
            out += [((0, -1), 1)]
        out += [((1, 0), 1), ((-1, 0), 1)]
    elif dy == 1 and dz in (0, 1, 2, 3):
        out += [((1, 0), 1)]
    elif dy == -1 and dz in (-1, -2, -3, 4):
        out += [((-1, 0), 1)]
    return out


def after(b, step, hops):
    dy, dz = b[0] + step[0] * hops, b[1] + step[1] * hops
    return (2 if dy == -2 else dy, 4 if dz == -4 else dz)


def split3(v):
    hi = v.astype(BF16).astype(F32)
    rest = v - hi
    mid = rest.astype(BF16).astype(F32)
    return hi, mid, rest - mid


def rows_of(parts, width):
    row = lax.broadcasted_iota(jnp.int32, (8, width), 0)
    out = jnp.zeros((8, width), F32)
    for i, part in enumerate(parts):
        out = jnp.where(row == i, jnp.broadcast_to(part, (8, width)), out)
    return out


def quotient(s):
    q = jnp.zeros_like(s)
    for i in range(1, NDP):
        q = q + (s >= BUCKET * i).astype(jnp.int32)
    return q


def spread(parts, q):
    return jnp.concatenate(
        [jnp.where(q == r, parts, 0.0) for r in range(NDP)], axis=0
    ).astype(BF16)


def collect(table, q):
    out = jnp.where(q == 0, table[0:8], 0.0)
    for r in range(1, NDP):
        out = out + jnp.where(q == r, table[8 * r : 8 * r + 8], 0.0)
    return out


def nt_dot(a, b):
    return lax.dot_general(a, b, (((1,), (1,)), ((), ())), preferred_element_type=F32)


def kernel(
    hid_hbm, gain_hbm, win_hbm, wout_hbm, rew_hbm, old_hbm, send_hbm, pack_hbm, pos_hbm, len_hbm,
    table_out,
    hid, wall, acc, ssq, inv, gain_in, win, wout, rew, old, send, pack, pos, elen,
    hot_send, hot_pack, osend, oland, rsend, rland, lev, tail_a, rowdat,
    first_a, esend, eland, weight, csend, cland, tsend, tland, isend, iland, own,
    sem_hid, sem_small, tree_recv, rest_recv, x_recv, sib_recv, sem_sent, sem_ex,
):
    dp = lax.axis_index("dp")
    ctx = lax.axis_index("context")
    y = lax.rem(ctx, NY)
    z = lax.div(ctx, NY)
    core = lax.rem(dp, 2)
    even = 1 - lax.rem(lax.div(dp, 2), 2)

    def ctx_at(dy, dz):
        return lax.rem(z + dz + NZ, NZ) * NY + lax.rem(y + dy + NY, NY)

    def dp_at(step):
        return lax.rem(dp + step + NDP, NDP)

    sibling = dp + 1 - 2 * core

    def at(dy, dz):
        return (dp, ctx_at(dy, dz))

    smalls = [
        (send_hbm, send), (rew_hbm, rew), (old_hbm, old), (pack_hbm, pack),
        (gain_hbm, gain_in), (pos_hbm, pos), (len_hbm, elen), (wout_hbm, wout), (win_hbm, win),
    ]
    small_copies = [
        pltpu.make_async_copy(src, dst, sem_small.at[i]) for i, (src, dst) in enumerate(smalls)
    ]
    small_copies[8].start()
    small_copies[4].start()

    barrier = pltpu.get_barrier_semaphore()

    peers = [at(k, 0) for k in range(1, NY)] + [at(0, k) for k in range(1, NZ)]
    peers += [(dp_at(k), ctx) for k in range(1, NDP)]
    for peer in peers:
        pl.semaphore_signal(barrier, inc=1, device_id=peer, device_id_type=MESH)
    for i in (0, 1, 2, 3, 5, 6, 7):
        small_copies[i].start()

    small_copies[4].wait()
    small_copies[8].wait()
    square = (KB, KB)
    diagonal = lax.broadcasted_iota(jnp.int32, square, 0) == lax.broadcasted_iota(
        jnp.int32, square, 1
    )
    gains = jnp.broadcast_to(gain_in[...].astype(F32).reshape(1, KB), square)
    wall[0] = jnp.dot(
        jnp.where(diagonal, gains, 0.0).astype(BF16), win[...], preferred_element_type=F32
    ).astype(BF16)

    def load(g):
        for j in range(GB):
            b = GROUPS[g][j]
            column = pl.multiple_of(ctx_at(-b[0], -b[1]) * KB, KB)
            pltpu.make_async_copy(
                hid_hbm.at[0, :, pl.ds(column, KB)], hid.at[g, :, pl.ds(j * KB, KB)], sem_hid.at[g]
            ).start()

    pl.semaphore_wait(barrier, len(peers))

    base = HALF * core
    rest_rows = pl.ds(pl.multiple_of(base + XR, 16), TREE - XR)
    x_rows = pl.ds(pl.multiple_of(base + TREE * even, 16), XR)
    x_lands = pl.ds(pl.multiple_of(base + TREE * (1 - even), 16), XR)
    half_rows = pl.ds(pl.multiple_of(base, 16), HALF)
    other_rows = pl.ds(pl.multiple_of(HALF - base, 16), HALF)
    x_peer = (dp_at(2 - 4 * core), ctx)

    def tree_step(c, b, first):
        slot = SLOT[b]
        rows = x_rows if first else rest_rows
        arrived = tree_recv if first else rest_recv
        if slot:
            here = wall.at[slot, rows]
            pltpu.make_async_copy(here, here, arrived.at[slot]).wait()
        for step, hops in (children_yz if c == 0 else children_zy)(*b):
            to = SLOT[after(b, step, hops)]
            pltpu.make_async_remote_copy(
                src_ref=wall.at[slot, rows],
                dst_ref=wall.at[to, rows],
                send_sem=sem_sent.at[0],
                recv_sem=arrived.at[to],
                device_id=at(step[0] * hops, step[1] * hops),
                device_id_type=MESH,
            ).start()
        if slot and first:
            part = wall.at[slot, x_rows]
            pltpu.make_async_remote_copy(
                src_ref=part,
                dst_ref=part,
                send_sem=sem_sent.at[1],
                recv_sem=x_recv.at[slot],
                device_id=x_peer,
                device_id_type=MESH,
            ).start()

    def x_step(slot):
        part = wall.at[slot, x_lands]
        pltpu.make_async_copy(part, part, x_recv.at[slot]).wait()

    def hand_over(slot):
        part = wall.at[slot, half_rows]
        pltpu.make_async_remote_copy(
            src_ref=part,
            dst_ref=part,
            send_sem=sem_sent.at[2],
            recv_sem=sib_recv.at[slot],
            device_id=(sibling, ctx),
            device_id_type=MESH,
        ).start()

    def handed(slot):
        part = wall.at[slot, other_rows]
        pltpu.make_async_copy(part, part, sib_recv.at[slot]).wait()

    seen = [set(), set()]

    def arrivals(c, codes):
        for code in codes:
            slot = code % 32
            if code // 32 == 1:
                x_step(slot)
            else:
                tree_step(c, BLOCKS[slot], code < 32)
            seen[c].add(code)
            if {slot, slot + 32, slot + 64} <= seen[c]:
                hand_over(slot)

    def by_core(first, second):
        if first:

            @pl.when(core == 0)
            def _():
                arrivals(0, first)

        if second:

            @pl.when(core == 1)
            def _():
                arrivals(1, second)

    def exchange(pairs, send_sem, recv_sem):
        for src, dst, device in pairs:
            pltpu.make_async_remote_copy(
                src_ref=src, dst_ref=dst, send_sem=send_sem, recv_sem=recv_sem,
                device_id=device, device_id_type=MESH,
            ).start()

    def await_bytes(ref, sem):
        pltpu.make_async_copy(ref, ref, sem).wait()

    def along_context(src, land, sem):
        def one(k, _):
            pltpu.make_async_remote_copy(
                src_ref=src, dst_ref=land.at[pl.ds(ctx, 1)],
                send_sem=sem_ex.at[sem], recv_sem=sem_ex.at[sem + 1],
                device_id=(dp, lax.rem(ctx + NY * NZ - k, NY * NZ)), device_id_type=MESH,
            ).start()
            return 0

        lax.fori_loop(1, NY * NZ, one, 0)

    def along_dp(src, dst, sem):
        exchange(
            [(src.at[dp_at(k)], dst, (dp_at(k), ctx)) for k in range(1, NDP)],
            sem_ex.at[sem],
            sem_ex.at[sem + 1],
        )

    def to_rows():
        for i in range(3):
            small_copies[i].wait()
        s = send[...]
        q = quotient(s)
        k = s - BUCKET * q
        hot_send[...] = (
            lax.broadcasted_iota(jnp.int32, (BW, S), 0) == jnp.broadcast_to(k, (BW, S))
        ).astype(F32).astype(BF16)
        parts = rows_of(split3(rew[...]) + split3(old[...]), S)
        table = nt_dot(spread(parts, q), hot_send[...])
        for r in range(NDP):
            osend[r] = table[8 * r : 8 * r + 8]
        along_dp(osend, oland.at[dp], 4)
        oland[pl.ds(dp, 1)] = osend[pl.ds(dp, 1)]

    def pack_table():
        small_copies[3].wait()
        s = pack[...]
        k = s - BUCKET * quotient(s)
        hot_pack[...] = (
            lax.broadcasted_iota(jnp.int32, (BW, T), 0) == jnp.broadcast_to(k, (BW, T))
        ).astype(F32).astype(BF16)

    def at_rows():
        await_bytes(oland.at[pl.ds(0, NDP - 1)], sem_ex.at[5])
        table = oland[...].reshape(8 * NDP, BW).astype(BF16)
        got = collect(
            jnp.dot(table, hot_pack[...], preferred_element_type=F32), quotient(pack[...])
        )
        rowdat[0] = jnp.broadcast_to(got[0:1] + got[1:2] + got[2:3], (8, T))
        rowdat[1] = jnp.broadcast_to(got[3:4] + got[4:5] + got[5:6], (8, T))

    lane = lax.broadcasted_iota(jnp.int32, (8, T), 1)
    row8 = lax.broadcasted_iota(jnp.int32, (8, T), 0)
    strides = [(1, 3), (4, 3), (16, 3), (64, 3), (256, 2)]

    def later(v, d, fill):
        return jnp.where(lane < T - d, pltpu.roll(v, T - d, 1), fill)

    def wide(slab):
        return jnp.concatenate([slab] * (T // 128), axis=1)

    def slab_of(v):
        return jnp.broadcast_to(v[:, 0:1], (8, 128))

    def coefficients():
        small_copies[5].wait()
        small_copies[6].wait()
        keep = jnp.where(pos[...] == 0, 0.0, 1.0).astype(F32)
        below = elen[...].astype(F32) + 20.0
        lost = 20.0 / below
        lost = lost + lost * (20.0 - lost * below) * 0.05
        keep8 = jnp.broadcast_to(keep, (8, T))
        lost8 = jnp.broadcast_to(lost, (8, T))
        rowdat[2] = keep8
        rowdat[3] = lost8
        a = jnp.where(row8 == 1, keep8, keep8 * (1.0 - lost8))
        i = 0
        for d, count in strides:
            reach = a
            for k in range(1, count + 1):
                lev[i] = jnp.where(lane < T - k * d, reach, 0.0)
                reach = reach * later(a, k * d, 1.0)
                i += 1
            a = reach
        tail_a[...] = later(a, 1, 1.0)
        first_a[...] = slab_of(a)

    def scan(b):
        i = 0
        for d, count in strides:
            total = b
            for k in range(1, count + 1):
                total = total + lev[i] * pltpu.roll(b, T - k * d, 1)
                i += 1
            b = total
        return b

    def tails():
        table = nt_dot(
            spread(rows_of(split3(tail_a[0:1]), T), quotient(pack[...])), hot_pack[...]
        )
        for r in range(NDP):
            tsend[r] = table[8 * r : 8 * r + 8]
        along_dp(tsend, tland.at[dp], 16)
        tland[pl.ds(dp, 1)] = tsend[pl.ds(dp, 1)]

    def to_owner(land):
        table = land[...].reshape(8 * NDP, BW).astype(BF16)
        return collect(
            jnp.dot(table, hot_send[...], preferred_element_type=F32), quotient(send[...])
        )

    def tails_in():
        await_bytes(tland.at[pl.ds(0, NDP - 1)], sem_ex.at[17])
        got = to_owner(tland)
        own[...] = jnp.zeros((8, S), F32)
        own[0:1] = got[0:1] + got[1:2] + got[2:3]

    def returns_scan():
        b = scan(jnp.where(row8 == 1, rowdat[2] * rowdat[0], 0.0))
        rowdat[4] = later(b, 1, 0.0)
        esend[0] = jnp.concatenate([first_a[0:1], first_a[1:2], slab_of(b)[1:2]], axis=1)
        eland[pl.ds(ctx, 1)] = esend[...]
        exchange(
            [(esend, eland.at[pl.ds(ctx, 1)], at(k, 0)) for k in range(1, NY)], sem_ex.at[6], sem_ex.at[7]
        )

    def carry_z():
        await_bytes(eland.at[pl.ds(0, NY - 1)], sem_ex.at[7])
        mine = eland.at[pl.ds(pl.multiple_of(z * NY, NY), NY)]
        exchange([(mine, mine, at(0, k)) for k in range(1, NZ)], sem_ex.at[8], sem_ex.at[9])

    def returns_done():
        await_bytes(eland.at[pl.ds(0, NY * (NZ - 1))], sem_ex.at[9])
        inflow = jnp.zeros((1, 128), F32)
        for i in reversed(range(NY * NZ)):
            inflow = jnp.where(
                i > ctx, eland[i, :, 256:384] + eland[i, :, 128:256] * inflow, inflow
            )
        reach = jnp.ones((1, 128), F32)
        for i in range(NY * NZ):
            weight[i] = jnp.where(i > ctx, reach, 0.0)
            reach = jnp.where(i > ctx, reach * eland[i, :, 0:128], reach)
        ret = rowdat[0] + tail_a[1:2] * wide(inflow) + rowdat[4]
        rowdat[5] = jnp.broadcast_to(ret[1:2], (8, T))
        keep8, lost8 = rowdat[2], rowdat[3]
        rowdat[6] = keep8 * (1.0 - lost8) * rowdat[0]
        rowdat[7] = keep8 * lost8

    TR = 32

    def over_rows(body, half):
        def one(i, _):
            body(pl.ds(pl.multiple_of(half * (T // 2) + i * TR, TR), TR))
            return 0

        lax.fori_loop(0, T // 2 // TR, one, 0)

    def squares(g, half):
        if half == 0:
            pltpu.make_async_copy(hid.at[g], hid.at[g], sem_hid.at[g]).wait()

        def body(rows):
            v = hid[g, rows, :].astype(F32)
            v = v * v
            total = v[:, 0:128]
            for j in range(1, KG // 128):
                total = total + v[:, 128 * j : 128 * j + 128]
            ssq[rows, :] = total if g == 0 else ssq[rows, :] + total

        over_rows(body, half)

    def inverse():
        def body(i, _):
            rows = pl.ds(pl.multiple_of(i * 128, 128), 128)
            mean = jnp.sum(ssq[rows, :], axis=1, keepdims=True) * (1.0 / D)
            inv[rows, :] = jnp.broadcast_to(lax.rsqrt(mean + EPS), (128, 128))
            return 0

        lax.fori_loop(0, T // 128, body, 0)

    def matmul(part, half, upper):
        first, end = PARTS[part]
        rows = slice(T // 2 * upper, T // 2 * upper + T // 2)
        if half == 0 and upper == 0:
            for slot in range(first, end):
                if slot:
                    handed(slot)
        cols = slice(256 * half, 256 * half + 256)
        w = wall[first:end, :, cols].reshape(KB * (end - first), 256)
        g, offset = divmod(first * KB, KG)
        v = jnp.dot(
            hid[g, rows, offset : offset + KB * (end - first)], w, preferred_element_type=F32
        )
        acc[rows, cols] = v if part == 0 else acc[rows, cols] + v

    items = dict(
        load=load, to_rows=to_rows, coefficients=coefficients, tails=tails,
        pack_table=pack_table, at_rows=at_rows, returns_scan=returns_scan, carry_z=carry_z,
        returns_done=returns_done, squares=squares, inverse=inverse,
        matmul=matmul, tails_in=tails_in,
    )
    for c in range(2):

        @pl.when(core == c)
        def _(c=c):
            tree_step(c, (0, 0), True)
            tree_step(c, (0, 0), False)

    for step in PLAN:
        if isinstance(step[0], str):
            items[step[0]](*step[1:])
        else:
            by_core(*step)

    for i in (7,):
        small_copies[i].wait()
    w_row = jnp.broadcast_to(wout[...].astype(F32).reshape(1, VH), (16, VH)).astype(BF16)

    def activate(i, _):
        rows = pl.ds(pl.multiple_of(i * 128, 128), 128)
        half = acc[rows, :] * jnp.concatenate([inv[rows, :] * 0.5] * (VH // 128), axis=1)
        act = (half * jnp.tanh(half) + half).astype(BF16)
        hid[0, rows, 0:VH] = act
        return 0

    lax.fori_loop(0, T // 128, activate, 0)
    values = nt_dot(w_row, hid[0, :, 0:VH])[0:8]

    b = scan(rowdat[7] * values + rowdat[6])
    csend[0] = slab_of(b)[0:1]
    along_context(csend, cland, 10)
    cland[pl.ds(ctx, 1)] = csend[...]
    base_adv = rowdat[0] - values + later(b, 1, 0.0)
    old_row, ret = rowdat[1], rowdat[5]
    clipped = old_row + jnp.clip(values - old_row, -0.2, 0.2)
    loss = 0.5 * jnp.maximum(jnp.square(values - ret), jnp.square(clipped - ret))
    parts = rows_of(split3(base_adv[0:1]) + split3(loss[0:1]), T)
    table = nt_dot(spread(parts, quotient(pack[...])), hot_pack[...])
    for r in range(NDP):
        rsend[r] = table[8 * r : 8 * r + 8]
    along_dp(rsend, rland.at[dp], 14)
    rland[pl.ds(dp, 1)] = rsend[pl.ds(dp, 1)]

    q = quotient(send[...])
    await_bytes(rland.at[pl.ds(0, NDP - 1)], sem_ex.at[15])
    got = to_owner(rland)
    own[1:2] = got[0:1] + got[1:2] + got[2:3]
    own[2:3] = got[3:4] + got[4:5]
    own[3:4] = got[5:6]
    await_bytes(cland.at[pl.ds(0, NY * NZ - 1)], sem_ex.at[11])
    inflow = weight[0] * cland[0]
    for i in range(1, NY * NZ):
        inflow = inflow + weight[i] * cland[i]
    inflow = jnp.broadcast_to(inflow, (8, 128))
    isend[...] = inflow
    iland[pl.ds(dp, 1)] = inflow[None]
    exchange(
        [(isend, iland.at[dp], (dp_at(k), ctx)) for k in range(1, NDP)], sem_ex.at[18], sem_ex.at[19]
    )

    await_bytes(wall.at[pl.ds(0, 31), pl.ds(0, TREE)], sem_sent.at[0])
    await_bytes(wall.at[pl.ds(0, 31), pl.ds(0, XR)], sem_sent.at[1])
    await_bytes(wall.at[pl.ds(0, 31), pl.ds(0, HALF)], sem_sent.at[2])
    await_bytes(oland.at[pl.ds(0, NDP - 1)], sem_ex.at[4])
    await_bytes(eland.at[pl.ds(0, NY - 1)], sem_ex.at[6])
    await_bytes(eland.at[pl.ds(0, NY * (NZ - 1))], sem_ex.at[8])
    await_bytes(cland.at[pl.ds(0, NY * NZ - 1)], sem_ex.at[10])
    await_bytes(rland.at[pl.ds(0, NDP - 1)], sem_ex.at[14])
    await_bytes(tland.at[pl.ds(0, NDP - 1)], sem_ex.at[16])

    await_bytes(iland.at[pl.ds(0, NDP - 1)], sem_ex.at[19])
    flow = jnp.zeros((1, S), F32)
    for r in range(NDP):
        here = jnp.concatenate([iland[r, 0:1]] * (S // 128), axis=1)
        flow = flow + jnp.where(q == r, here, 0.0)
    own[0:1] = own[0:1] * flow
    table_copy = pltpu.make_async_copy(own, table_out, sem_small.at[0])
    table_copy.start()
    await_bytes(iland.at[pl.ds(0, NDP - 1)], sem_ex.at[18])
    table_copy.wait()


def local(
    hidden, norm_gain, w_in, w_out, rewards, old_values, send_slot, pack_slot, positions, episode_len
):
    outside = pl.BlockSpec(memory_space=pltpu.HBM)
    vmem = pltpu.VMEM
    dma = pltpu.SemaphoreType.DMA
    table = pl.pallas_call(
        kernel,
        out_shape=jax.ShapeDtypeStruct((8, S), F32),
        in_specs=[outside] * 10,
        out_specs=outside,
        scratch_shapes=[
            vmem((NG, T, KG), BF16),
            vmem((NY * NZ, KB, VH), BF16),
            vmem((T, VH), F32),
            vmem((T, 128), F32),
            vmem((T, 128), F32),
            vmem((KB,), BF16),
            vmem((KB, VH), BF16),
            vmem((VH,), BF16),
            vmem((1, S), F32),
            vmem((1, S), F32),
            vmem((1, S), jnp.int32),
            vmem((1, T), jnp.int32),
            vmem((1, T), jnp.int32),
            vmem((1, T), jnp.int32),
            vmem((BW, S), BF16),
            vmem((BW, T), BF16),
            vmem((NDP, 8, BW), F32),
            vmem((NDP, 8, BW), F32),
            vmem((NDP, 8, BW), F32),
            vmem((NDP, 8, BW), F32),
            vmem((14, 8, T), F32),
            vmem((8, T), F32),
            vmem((8, 8, T), F32),
            vmem((8, 128), F32),
            vmem((1, 1, 384), F32),
            vmem((NY * NZ, 1, 384), F32),
            vmem((NY * NZ, 1, 128), F32),
            vmem((1, 1, 128), F32),
            vmem((NY * NZ, 1, 128), F32),
            vmem((NDP, 8, BW), F32),
            vmem((NDP, 8, BW), F32),
            vmem((8, 128), F32),
            vmem((NDP, 8, 128), F32),
            vmem((8, S), F32),
            dma((NG,)),
            dma((9,)),
            dma((NY * NZ,)),
            dma((NY * NZ,)),
            dma((NY * NZ,)),
            dma((NY * NZ,)),
            dma((3,)),
            dma((20,)),
        ],
        compiler_params=pltpu.CompilerParams(
            collective_id=0, has_side_effects=True, vmem_limit_bytes=63 * 1024 * 1024
        ),
        name="critic",
    )(
        hidden,
        norm_gain,
        w_in,
        w_out,
        rewards,
        old_values,
        send_slot,
        pack_slot,
        positions,
        episode_len,
    )
    return table[0:1] + table[1:2], table[2:3] + table[3:4]


def solution(mesh):
    both = P("dp", "context")
    return jax.shard_map(
        local,
        mesh=mesh,
        in_specs=(P("dp", "context", None), P("context"), P("context", None), P()) + (both,) * 6,
        out_specs=(both, both),
        check_vma=False,
    )
```

```python
import jax
import jax.numpy as jnp
from jax import lax
from jax.experimental import pallas as pl
from jax.experimental.pallas import tpu as pltpu
from jax.sharding import PartitionSpec as P

F32 = jnp.float32
BF16 = jnp.bfloat16
MESH = pl.DeviceIdType.MESH

NX, NY, NZ = 4, 4, 8
NDP = 2 * NX
T = 768
S = 1536
D = 8192
VH = 512
KB = 256
BUCKET = 192
BW = 256
GB = 4
NG = 8
KG = GB * KB
EPS = 1e-05

HALF = KB // 2
XR = 48
TREE = HALF - XR

BLOCKS = [
    (0, 0), (-1, 0), (0, 1), (0, -1), (1, 0), (0, 2), (0, -2), (1, 1),
    (-1, 1), (1, -2), (1, -1), (-1, -2), (-1, -1), (0, -3), (2, 0), (1, 2),
    (-1, 2), (2, -2), (0, 3), (2, 1), (2, 2), (-1, -3), (1, -3), (2, -1),
    (0, 4), (1, 4), (1, 3), (-1, 3), (2, -3), (-1, 4), (2, 3), (2, 4),
]
GROUPS = [BLOCKS[GB * g : GB * g + GB] for g in range(NG)]
SLOT = {b: i for i, b in enumerate(BLOCKS)}
PARTS = [(GB * g, GB * g + GB) for g in range(NG - 1)] + [(28, 30), (30, 32)]

PLAN = [
    ('load', 0),
    ('load', 1),
    ('load', 2),
    ('load', 3),
    ('load', 4),
    ('load', 5),
    ('load', 6),
    ('load', 7),
    ('to_rows',),
    ('coefficients',),
    ('pack_table',),
    ('tails',),
    ((4,), ()),
    ((1, 2, 3), ()),
    ((65, 66, 67), ()),
    ('squares', 0, 0),
    ('squares', 0, 1),
    ((), (1,)),
    ((), (65,)),
    ((68,), ()),
    ((14,), ()),
    ('squares', 1, 0),
    ('squares', 1, 1),
    ((), (5,)),
    ((), (6, 2, 3)),
    ((78,), ()),
    ('squares', 2, 0),
    ((), (4,)),
    ('squares', 2, 1),
    ((), (68,)),
    ((), (66, 67)),
    ((), (69, 70)),
    ((7,), ()),
    ((10,), ()),
    ('squares', 3, 0),
    ((36,), ()),
    ('squares', 3, 1),
    ((8, 12), ()),
    ('at_rows',),
    ((33, 5, 6), ()),
    ((34, 72, 76), ()),
    ('returns_scan',),
    ((35, 69, 70), ()),
    ((71, 74), ()),
    ('squares', 4, 0),
    ((46,), ()),
    ('squares', 4, 1),
    ((19, 23), (33,)),
    ('squares', 5, 0),
    ('squares', 5, 1),
    ('squares', 6, 0),
    ((87,), (15, 16)),
    ('squares', 6, 1),
    ((), (37,)),
    ((), (9,)),
    ((), (11,)),
    ((), (38,)),
    ((), (7,)),
    ((), (8, 13)),
    ((), (34,)),
    ((), (10,)),
    ((), (12,)),
    ((), (77,)),
    ((), (35, 72)),
    ((), (14,)),
    ((), (24, 18)),
    ((), (36, 76, 78)),
    ('squares', 7, 0),
    ((39,), (80, 71)),
    ('squares', 7, 1),
    ((), (75, 74)),
    ('inverse',),
    ((42, 9, 83), (79, 82)),
    ((), (88,)),
    ((), (73,)),
    ('matmul', 0, 0, 0),
    ((40, 11, 44, 13, 75), (47, 17)),
    ((15, 77), (20,)),
    ((37,), ()),
    ('matmul', 0, 0, 1),
    ((73,), (48,)),
    ((16,), ()),
    ((38,), ()),
    ('matmul', 0, 1, 0),
    ((17,), (19, 21)),
    ((18,), (41,)),
    ((51,), ()),
    ((81,), ()),
    ((80,), ()),
    ('matmul', 0, 1, 1),
    ((55, 82), (22, 23)),
    ('carry_z',),
    ((), (43, 86)),
    ((), (85,)),
    ('tails_in',),
    ((79, 22), (39, 25, 29)),
    ((), (40,)),
    ((20,), ()),
    ((41,), ()),
    ((), (26,)),
    ((), (27,)),
    ((84,), ()),
    ((), (83,)),
    ((), (45, 87)),
    ((), (84,)),
    ((), (81,)),
    ((21,), ()),
    ((), (42,)),
    ((), (90,)),
    ((), (91,)),
    ('matmul', 1, 0, 0),
    ((43, 26, 85), (44, 89, 93)),
    ((86,), ()),
    ((27,), ()),
    ((45,), ()),
    ('matmul', 1, 0, 1),
    ((28,), (46, 28)),
    ((47, 24), ()),
    ('matmul', 1, 1, 0),
    ((92, 91), ()),
    ('matmul', 1, 1, 1),
    ((48, 88), (56, 92)),
    ('matmul', 2, 0, 0),
    ((49, 90), (50,)),
    ('matmul', 2, 0, 1),
    ((25,), (31,)),
    ((50, 30), (49,)),
    ('matmul', 2, 1, 0),
    ((94,), (30,)),
    ((54,), ()),
    ('matmul', 2, 1, 1),
    ((29,), (52,)),
    ('matmul', 3, 0, 0),
    ((52, 93), (51, 94)),
    ('matmul', 3, 0, 1),
    ((53, 89), ()),
    ('matmul', 3, 1, 0),
    ((), (53, 95)),
    ('matmul', 3, 1, 1),
    ((58, 31), ()),
    ((), (54,)),
    ((), (55,)),
    ((95,), ()),
    ('matmul', 4, 0, 0),
    ((59,), ()),
    ('matmul', 4, 0, 1),
    ((60,), ()),
    ('returns_done',),
    ((), (57,)),
    ('matmul', 4, 1, 0),
    ((56,), (61,)),
    ('matmul', 4, 1, 1),
    ((57,), ()),
    ('matmul', 5, 0, 0),
    ((), (58,)),
    ('matmul', 5, 0, 1),
    ((62,), (59,)),
    ('matmul', 5, 1, 0),
    ((61,), ()),
    ('matmul', 5, 1, 1),
    ((), (60,)),
    ((), (63,)),
    ((), (62,)),
    ((63,), ()),
    ('matmul', 6, 0, 0),
    ('matmul', 6, 0, 1),
    ('matmul', 6, 1, 0),
    ('matmul', 6, 1, 1),
    ('matmul', 7, 0, 0),
    ('matmul', 7, 0, 1),
    ('matmul', 7, 1, 0),
    ('matmul', 7, 1, 1),
    ('matmul', 8, 0, 0),
    ('matmul', 8, 0, 1),
    ('matmul', 8, 1, 0),
    ('matmul', 8, 1, 1),
]


def children_yz(dy, dz):
    out = []
    if dz == 0 and dy == 0:
        out += [((1, 0), 1), ((-1, 0), 1), ((1, 0), 2)]
    if dz in (0, 1, 2) or (dz == 3 and dy == 0):
        out += [((0, 1), 1)]
    if dz in (0, -1, -2) or (dz == -3 and dy != 0):
        out += [((0, -1), 1)]
    return out


def children_zy(dy, dz):
    out = []
    if dy == 0:
        if dz == 0:
            out += [((0, 1), 2), ((0, -1), 2), ((0, 1), 1), ((0, -1), 1)]
        elif dz == 2:
            out += [((0, 1), 2), ((0, 1), 1)]
        elif dz == -2:
            out += [((0, -1), 1)]
        out += [((1, 0), 1), ((-1, 0), 1)]
    elif dy == 1 and dz in (0, 1, 2, 3):
        out += [((1, 0), 1)]
    elif dy == -1 and dz in (-1, -2, -3, 4):
        out += [((-1, 0), 1)]
    return out


def after(b, step, hops):
    dy, dz = b[0] + step[0] * hops, b[1] + step[1] * hops
    return (2 if dy == -2 else dy, 4 if dz == -4 else dz)


def split3(v):
    hi = v.astype(BF16).astype(F32)
    rest = v - hi
    mid = rest.astype(BF16).astype(F32)
    return hi, mid, rest - mid


def rows_of(parts, width):
    row = lax.broadcasted_iota(jnp.int32, (8, width), 0)
    out = jnp.zeros((8, width), F32)
    for i, part in enumerate(parts):
        out = jnp.where(row == i, jnp.broadcast_to(part, (8, width)), out)
    return out


def quotient(s):
    q = jnp.zeros_like(s)
    for i in range(1, NDP):
        q = q + (s >= BUCKET * i).astype(jnp.int32)
    return q


def spread(parts, q):
    return jnp.concatenate(
        [jnp.where(q == r, parts, 0.0) for r in range(NDP)], axis=0
    ).astype(BF16)


def collect(table, q):
    out = jnp.where(q == 0, table[0:8], 0.0)
    for r in range(1, NDP):
        out = out + jnp.where(q == r, table[8 * r : 8 * r + 8], 0.0)
    return out


def nt_dot(a, b):
    return lax.dot_general(a, b, (((1,), (1,)), ((), ())), preferred_element_type=F32)


def kernel(
    hid_hbm, gain_hbm, win_hbm, wout_hbm, rew_hbm, old_hbm, send_hbm, pack_hbm, pos_hbm, len_hbm,
    table_out,
    hid, wall, acc, ssq, inv, gain_in, win, wout, rew, old, send, pack, pos, elen,
    hot_send, hot_pack, osend, oland, rsend, rland, lev, tail_a, rowdat,
    first_a, esend, eland, weight, csend, cland, tsend, tland, isend, iland, own,
    sem_hid, sem_small, tree_recv, rest_recv, x_recv, sib_recv, sem_sent, sem_ex,
):
    dp = lax.axis_index("dp")
    ctx = lax.axis_index("context")
    y = lax.rem(ctx, NY)
    z = lax.div(ctx, NY)
    core = lax.rem(dp, 2)
    even = 1 - lax.rem(lax.div(dp, 2), 2)

    def ctx_at(dy, dz):
        return lax.rem(z + dz + NZ, NZ) * NY + lax.rem(y + dy + NY, NY)

    def dp_at(step):
        return lax.rem(dp + step + NDP, NDP)

    sibling = dp + 1 - 2 * core

    def at(dy, dz):
        return (dp, ctx_at(dy, dz))

    smalls = [
        (send_hbm, send), (rew_hbm, rew), (old_hbm, old), (pack_hbm, pack),
        (gain_hbm, gain_in), (pos_hbm, pos), (len_hbm, elen), (wout_hbm, wout), (win_hbm, win),
    ]
    small_copies = [
        pltpu.make_async_copy(src, dst, sem_small.at[i]) for i, (src, dst) in enumerate(smalls)
    ]
    small_copies[8].start()
    small_copies[4].start()

    barrier = pltpu.get_barrier_semaphore()

    peers = [at(k, 0) for k in range(1, NY)] + [at(0, k) for k in range(1, NZ)]
    peers += [(dp_at(k), ctx) for k in range(1, NDP)]
    for peer in peers:
        pl.semaphore_signal(barrier, inc=1, device_id=peer, device_id_type=MESH)
    for i in (0, 1, 2, 3, 5, 6, 7):
        small_copies[i].start()

    small_copies[4].wait()
    small_copies[8].wait()
    square = (KB, KB)
    diagonal = lax.broadcasted_iota(jnp.int32, square, 0) == lax.broadcasted_iota(
        jnp.int32, square, 1
    )
    gains = jnp.broadcast_to(gain_in[...].astype(F32).reshape(1, KB), square)
    wall[0] = jnp.dot(
        jnp.where(diagonal, gains, 0.0).astype(BF16), win[...], preferred_element_type=F32
    ).astype(BF16)

    def load(g):
        for j in range(GB):
            b = GROUPS[g][j]
            column = pl.multiple_of(ctx_at(-b[0], -b[1]) * KB, KB)
            pltpu.make_async_copy(
                hid_hbm.at[0, :, pl.ds(column, KB)], hid.at[g, :, pl.ds(j * KB, KB)], sem_hid.at[g]
            ).start()

    pl.semaphore_wait(barrier, len(peers))

    base = HALF * core
    rest_rows = pl.ds(pl.multiple_of(base + XR, 16), TREE - XR)
    x_rows = pl.ds(pl.multiple_of(base + TREE * even, 16), XR)
    x_lands = pl.ds(pl.multiple_of(base + TREE * (1 - even), 16), XR)
    half_rows = pl.ds(pl.multiple_of(base, 16), HALF)
    other_rows = pl.ds(pl.multiple_of(HALF - base, 16), HALF)
    x_peer = (dp_at(2 - 4 * core), ctx)

    def tree_step(c, b, first):
        slot = SLOT[b]
        rows = x_rows if first else rest_rows
        arrived = tree_recv if first else rest_recv
        if slot:
            here = wall.at[slot, rows]
            pltpu.make_async_copy(here, here, arrived.at[slot]).wait()
        for step, hops in (children_yz if c == 0 else children_zy)(*b):
            to = SLOT[after(b, step, hops)]
            pltpu.make_async_remote_copy(
                src_ref=wall.at[slot, rows],
                dst_ref=wall.at[to, rows],
                send_sem=sem_sent.at[0],
                recv_sem=arrived.at[to],
                device_id=at(step[0] * hops, step[1] * hops),
                device_id_type=MESH,
            ).start()
        if slot and first:
            part = wall.at[slot, x_rows]
            pltpu.make_async_remote_copy(
                src_ref=part,
                dst_ref=part,
                send_sem=sem_sent.at[1],
                recv_sem=x_recv.at[slot],
                device_id=x_peer,
                device_id_type=MESH,
            ).start()

    def x_step(slot):
        part = wall.at[slot, x_lands]
        pltpu.make_async_copy(part, part, x_recv.at[slot]).wait()

    def hand_over(slot):
        part = wall.at[slot, half_rows]
        pltpu.make_async_remote_copy(
            src_ref=part,
            dst_ref=part,
            send_sem=sem_sent.at[2],
            recv_sem=sib_recv.at[slot],
            device_id=(sibling, ctx),
            device_id_type=MESH,
        ).start()

    def handed(slot):
        part = wall.at[slot, other_rows]
        pltpu.make_async_copy(part, part, sib_recv.at[slot]).wait()

    seen = [set(), set()]

    def arrivals(c, codes):
        for code in codes:
            slot = code % 32
            if code // 32 == 1:
                x_step(slot)
            else:
                tree_step(c, BLOCKS[slot], code < 32)
            seen[c].add(code)
            if {slot, slot + 32, slot + 64} <= seen[c]:
                hand_over(slot)

    def by_core(first, second):
        if first:

            @pl.when(core == 0)
            def _():
                arrivals(0, first)

        if second:

            @pl.when(core == 1)
            def _():
                arrivals(1, second)

    def exchange(pairs, send_sem, recv_sem):
        for src, dst, device in pairs:
            pltpu.make_async_remote_copy(
                src_ref=src, dst_ref=dst, send_sem=send_sem, recv_sem=recv_sem,
                device_id=device, device_id_type=MESH,
            ).start()

    def await_bytes(ref, sem):
        pltpu.make_async_copy(ref, ref, sem).wait()

    def along_context(src, land, sem):
        def one(k, _):
            pltpu.make_async_remote_copy(
                src_ref=src, dst_ref=land.at[pl.ds(ctx, 1)],
                send_sem=sem_ex.at[sem], recv_sem=sem_ex.at[sem + 1],
                device_id=(dp, lax.rem(ctx + NY * NZ - k, NY * NZ)), device_id_type=MESH,
            ).start()
            return 0

        lax.fori_loop(1, NY * NZ, one, 0)

    def along_dp(src, dst, sem):
        exchange(
            [(src.at[dp_at(k)], dst, (dp_at(k), ctx)) for k in range(1, NDP)],
            sem_ex.at[sem],
            sem_ex.at[sem + 1],
        )

    def to_rows():
        for i in range(3):
            small_copies[i].wait()
        s = send[...]
        q = quotient(s)
        k = s - BUCKET * q
        hot_send[...] = (
            lax.broadcasted_iota(jnp.int32, (BW, S), 0) == jnp.broadcast_to(k, (BW, S))
        ).astype(F32).astype(BF16)
        parts = rows_of(split3(rew[...]) + split3(old[...]), S)
        table = nt_dot(spread(parts, q), hot_send[...])
        for r in range(NDP):
            osend[r] = table[8 * r : 8 * r + 8]
        along_dp(osend, oland.at[dp], 4)
        oland[pl.ds(dp, 1)] = osend[pl.ds(dp, 1)]

    def pack_table():
        small_copies[3].wait()
        s = pack[...]
        k = s - BUCKET * quotient(s)
        hot_pack[...] = (
            lax.broadcasted_iota(jnp.int32, (BW, T), 0) == jnp.broadcast_to(k, (BW, T))
        ).astype(F32).astype(BF16)

    def at_rows():
        await_bytes(oland.at[pl.ds(0, NDP - 1)], sem_ex.at[5])
        table = oland[...].reshape(8 * NDP, BW).astype(BF16)
        got = collect(
            jnp.dot(table, hot_pack[...], preferred_element_type=F32), quotient(pack[...])
        )
        rowdat[0] = jnp.broadcast_to(got[0:1] + got[1:2] + got[2:3], (8, T))
        rowdat[1] = jnp.broadcast_to(got[3:4] + got[4:5] + got[5:6], (8, T))

    lane = lax.broadcasted_iota(jnp.int32, (8, T), 1)
    row8 = lax.broadcasted_iota(jnp.int32, (8, T), 0)
    strides = [(1, 3), (4, 3), (16, 3), (64, 3), (256, 2)]

    def later(v, d, fill):
        return jnp.where(lane < T - d, pltpu.roll(v, T - d, 1), fill)

    def wide(slab):
        return jnp.concatenate([slab] * (T // 128), axis=1)

    def slab_of(v):
        return jnp.broadcast_to(v[:, 0:1], (8, 128))

    def coefficients():
        small_copies[5].wait()
        small_copies[6].wait()
        keep = jnp.where(pos[...] == 0, 0.0, 1.0).astype(F32)
        below = elen[...].astype(F32) + 20.0
        lost = 20.0 / below
        lost = lost + lost * (20.0 - lost * below) * 0.05
        keep8 = jnp.broadcast_to(keep, (8, T))
        lost8 = jnp.broadcast_to(lost, (8, T))
        rowdat[2] = keep8
        rowdat[3] = lost8
        a = jnp.where(row8 == 1, keep8, keep8 * (1.0 - lost8))
        i = 0
        for d, count in strides:
            reach = a
            for k in range(1, count + 1):
                lev[i] = jnp.where(lane < T - k * d, reach, 0.0)
                reach = reach * later(a, k * d, 1.0)
                i += 1
            a = reach
        tail_a[...] = later(a, 1, 1.0)
        first_a[...] = slab_of(a)

    def scan(b):
        i = 0
        for d, count in strides:
            total = b
            for k in range(1, count + 1):
                total = total + lev[i] * pltpu.roll(b, T - k * d, 1)
                i += 1
            b = total
        return b

    def tails():
        table = nt_dot(
            spread(rows_of(split3(tail_a[0:1]), T), quotient(pack[...])), hot_pack[...]
        )
        for r in range(NDP):
            tsend[r] = table[8 * r : 8 * r + 8]
        along_dp(tsend, tland.at[dp], 16)
        tland[pl.ds(dp, 1)] = tsend[pl.ds(dp, 1)]

    def to_owner(land):
        table = land[...].reshape(8 * NDP, BW).astype(BF16)
        return collect(
            jnp.dot(table, hot_send[...], preferred_element_type=F32), quotient(send[...])
        )

    def tails_in():
        await_bytes(tland.at[pl.ds(0, NDP - 1)], sem_ex.at[17])
        got = to_owner(tland)
        own[0] = got[0:1] + got[1:2] + got[2:3]

    def returns_scan():
        b = scan(jnp.where(row8 == 1, rowdat[2] * rowdat[0], 0.0))
        rowdat[4] = later(b, 1, 0.0)
        esend[0] = jnp.concatenate([first_a[0:1], first_a[1:2], slab_of(b)[1:2]], axis=1)
        eland[pl.ds(ctx, 1)] = esend[...]
        exchange(
            [(esend, eland.at[pl.ds(ctx, 1)], at(k, 0)) for k in range(1, NY)], sem_ex.at[6], sem_ex.at[7]
        )

    def carry_z():
        await_bytes(eland.at[pl.ds(0, NY - 1)], sem_ex.at[7])
        mine = eland.at[pl.ds(pl.multiple_of(z * NY, NY), NY)]
        exchange([(mine, mine, at(0, k)) for k in range(1, NZ)], sem_ex.at[8], sem_ex.at[9])

    def returns_done():
        await_bytes(eland.at[pl.ds(0, NY * (NZ - 1))], sem_ex.at[9])
        inflow = jnp.zeros((1, 128), F32)
        for i in reversed(range(NY * NZ)):
            inflow = jnp.where(
                i > ctx, eland[i, :, 256:384] + eland[i, :, 128:256] * inflow, inflow
            )
        reach = jnp.ones((1, 128), F32)
        for i in range(NY * NZ):
            weight[i] = jnp.where(i > ctx, reach, 0.0)
            reach = jnp.where(i > ctx, reach * eland[i, :, 0:128], reach)
        ret = rowdat[0] + tail_a[1:2] * wide(inflow) + rowdat[4]
        rowdat[5] = jnp.broadcast_to(ret[1:2], (8, T))
        keep8, lost8 = rowdat[2], rowdat[3]
        rowdat[6] = keep8 * (1.0 - lost8) * rowdat[0]
        rowdat[7] = keep8 * lost8

    TR = 32

    def over_rows(body, half):
        def one(i, _):
            body(pl.ds(pl.multiple_of(half * (T // 2) + i * TR, TR), TR))
            return 0

        lax.fori_loop(0, T // 2 // TR, one, 0)

    def squares(g, half):
        if half == 0:
            pltpu.make_async_copy(hid.at[g], hid.at[g], sem_hid.at[g]).wait()

        def body(rows):
            v = hid[g, rows, :].astype(F32)
            v = v * v
            total = v[:, 0:128]
            for j in range(1, KG // 128):
                total = total + v[:, 128 * j : 128 * j + 128]
            ssq[rows, :] = total if g == 0 else ssq[rows, :] + total

        over_rows(body, half)

    def inverse():
        def body(i, _):
            rows = pl.ds(pl.multiple_of(i * 128, 128), 128)
            mean = jnp.sum(ssq[rows, :], axis=1, keepdims=True) * (1.0 / D)
            inv[rows, :] = jnp.broadcast_to(lax.rsqrt(mean + EPS), (128, 128))
            return 0

        lax.fori_loop(0, T // 128, body, 0)

    def matmul(part, half, upper):
        first, end = PARTS[part]
        rows = slice(T // 2 * upper, T // 2 * upper + T // 2)
        if half == 0 and upper == 0:
            for slot in range(first, end):
                if slot:
                    handed(slot)
        cols = slice(256 * half, 256 * half + 256)
        w = wall[first:end, :, cols].reshape(KB * (end - first), 256)
        g, offset = divmod(first * KB, KG)
        v = jnp.dot(
            hid[g, rows, offset : offset + KB * (end - first)], w, preferred_element_type=F32
        )
        acc[rows, cols] = v if part == 0 else acc[rows, cols] + v

    items = dict(
        load=load, to_rows=to_rows, coefficients=coefficients, tails=tails,
        pack_table=pack_table, at_rows=at_rows, returns_scan=returns_scan, carry_z=carry_z,
        returns_done=returns_done, squares=squares, inverse=inverse,
        matmul=matmul, tails_in=tails_in,
    )
    for c in range(2):

        @pl.when(core == c)
        def _(c=c):
            tree_step(c, (0, 0), True)
            tree_step(c, (0, 0), False)

    for step in PLAN:
        if isinstance(step[0], str):
            items[step[0]](*step[1:])
        else:
            by_core(*step)

    for i in (7,):
        small_copies[i].wait()
    w_row = jnp.broadcast_to(wout[...].astype(F32).reshape(1, VH), (16, VH)).astype(BF16)

    def activate(i, _):
        rows = pl.ds(pl.multiple_of(i * 128, 128), 128)
        half = acc[rows, :] * jnp.concatenate([inv[rows, :] * 0.5] * (VH // 128), axis=1)
        act = (half * jnp.tanh(half) + half).astype(BF16)
        hid[0, rows, 0:VH] = act
        return 0

    lax.fori_loop(0, T // 128, activate, 0)
    values = nt_dot(w_row, hid[0, :, 0:VH])[0:8]

    b = scan(rowdat[7] * values + rowdat[6])
    csend[0] = slab_of(b)[0:1]
    along_context(csend, cland, 10)
    cland[pl.ds(ctx, 1)] = csend[...]
    base_adv = rowdat[0] - values + later(b, 1, 0.0)
    old_row, ret = rowdat[1], rowdat[5]
    clipped = old_row + jnp.clip(values - old_row, -0.2, 0.2)
    loss = 0.5 * jnp.maximum(jnp.square(values - ret), jnp.square(clipped - ret))
    parts = rows_of(split3(base_adv[0:1]) + split3(loss[0:1]), T)
    table = nt_dot(spread(parts, quotient(pack[...])), hot_pack[...])
    for r in range(NDP):
        rsend[r] = table[8 * r : 8 * r + 8]
    along_dp(rsend, rland.at[dp], 14)
    rland[pl.ds(dp, 1)] = rsend[pl.ds(dp, 1)]

    q = quotient(send[...])
    await_bytes(rland.at[pl.ds(0, NDP - 1)], sem_ex.at[15])
    got = to_owner(rland)
    own[1] = got[0:1] + got[1:2] + got[2:3]
    own[2] = got[3:4] + got[4:5]
    own[3] = got[5:6]
    await_bytes(cland.at[pl.ds(0, NY * NZ - 1)], sem_ex.at[11])
    inflow = weight[0] * cland[0]
    for i in range(1, NY * NZ):
        inflow = inflow + weight[i] * cland[i]
    inflow = jnp.broadcast_to(inflow, (8, 128))
    isend[...] = inflow
    iland[pl.ds(dp, 1)] = inflow[None]
    exchange(
        [(isend, iland.at[dp], (dp_at(k), ctx)) for k in range(1, NDP)], sem_ex.at[18], sem_ex.at[19]
    )

    await_bytes(wall.at[pl.ds(0, 31), pl.ds(0, TREE)], sem_sent.at[0])
    await_bytes(wall.at[pl.ds(0, 31), pl.ds(0, XR)], sem_sent.at[1])
    await_bytes(wall.at[pl.ds(0, 31), pl.ds(0, HALF)], sem_sent.at[2])
    await_bytes(oland.at[pl.ds(0, NDP - 1)], sem_ex.at[4])
    await_bytes(eland.at[pl.ds(0, NY - 1)], sem_ex.at[6])
    await_bytes(eland.at[pl.ds(0, NY * (NZ - 1))], sem_ex.at[8])
    await_bytes(cland.at[pl.ds(0, NY * NZ - 1)], sem_ex.at[10])
    await_bytes(rland.at[pl.ds(0, NDP - 1)], sem_ex.at[14])
    await_bytes(tland.at[pl.ds(0, NDP - 1)], sem_ex.at[16])

    await_bytes(iland.at[pl.ds(0, NDP - 1)], sem_ex.at[19])
    flow = jnp.zeros((1, S), F32)
    for r in range(NDP):
        here = jnp.concatenate([iland[r, 0:1]] * (S // 128), axis=1)
        flow = flow + jnp.where(q == r, here, 0.0)
    own[0] = own[0] * flow
    table_copy = pltpu.make_async_copy(own, table_out, sem_small.at[0])
    table_copy.start()
    await_bytes(iland.at[pl.ds(0, NDP - 1)], sem_ex.at[18])
    table_copy.wait()


def local(
    hidden, norm_gain, w_in, w_out, rewards, old_values, send_slot, pack_slot, positions, episode_len
):
    outside = pl.BlockSpec(memory_space=pltpu.HBM)
    vmem = pltpu.VMEM
    dma = pltpu.SemaphoreType.DMA
    table = pl.pallas_call(
        kernel,
        out_shape=jax.ShapeDtypeStruct((4, 1, S), F32),
        in_specs=[outside] * 10,
        out_specs=outside,
        scratch_shapes=[
            vmem((NG, T, KG), BF16),
            vmem((NY * NZ, KB, VH), BF16),
            vmem((T, VH), F32),
            vmem((T, 128), F32),
            vmem((T, 128), F32),
            vmem((KB,), BF16),
            vmem((KB, VH), BF16),
            vmem((VH,), BF16),
            vmem((1, S), F32),
            vmem((1, S), F32),
            vmem((1, S), jnp.int32),
            vmem((1, T), jnp.int32),
            vmem((1, T), jnp.int32),
            vmem((1, T), jnp.int32),
            vmem((BW, S), BF16),
            vmem((BW, T), BF16),
            vmem((NDP, 8, BW), F32),
            vmem((NDP, 8, BW), F32),
            vmem((NDP, 8, BW), F32),
            vmem((NDP, 8, BW), F32),
            vmem((14, 8, T), F32),
            vmem((8, T), F32),
            vmem((8, 8, T), F32),
            vmem((8, 128), F32),
            vmem((1, 1, 384), F32),
            vmem((NY * NZ, 1, 384), F32),
            vmem((NY * NZ, 1, 128), F32),
            vmem((1, 1, 128), F32),
            vmem((NY * NZ, 1, 128), F32),
            vmem((NDP, 8, BW), F32),
            vmem((NDP, 8, BW), F32),
            vmem((8, 128), F32),
            vmem((NDP, 8, 128), F32),
            vmem((4, 1, S), F32),
            dma((NG,)),
            dma((9,)),
            dma((NY * NZ,)),
            dma((NY * NZ,)),
            dma((NY * NZ,)),
            dma((NY * NZ,)),
            dma((3,)),
            dma((20,)),
        ],
        compiler_params=pltpu.CompilerParams(
            collective_id=0, has_side_effects=True, vmem_limit_bytes=63 * 1024 * 1024
        ),
        name="critic",
    )(
        hidden,
        norm_gain,
        w_in,
        w_out,
        rewards,
        old_values,
        send_slot,
        pack_slot,
        positions,
        episode_len,
    )
    return table[0] + table[1], table[2] + table[3]


def solution(mesh):
    both = P("dp", "context")
    return jax.shard_map(
        local,
        mesh=mesh,
        in_specs=(P("dp", "context", None), P("context"), P("context", None), P()) + (both,) * 6,
        out_specs=(both, both),
        check_vma=False,
    )
```
